32 devices in a mesh: groups: 1, pts: 32 (over z, y, x, core).
Axes of the slice: x: 2, y: 2, z: 4, core: 2. Of those that a mesh axis runs over, the one named last changes fastest.
Arguments:
- residual_cols: bfloat16 [16384, 256], P(('groups', 'pts')), may hold values from -6 to 6
- leaf_inverse: bfloat16 [16384, 128], P(('groups', 'pts'))
- basis_left: float32 [7, 16384, 128], P(None, ('groups', 'pts')), may hold values from -0.15625 to 0.15625
- basis_right: float32 [7, 16384, 128], P(None, ('groups', 'pts'))
- point_pos: float32 [16384], replicated, may hold values from 0 to 16, as said below
- map_pos: float32 [2048], P('pts'), may hold values from 0 to 16, as said below
- prior_map: bfloat16 [2048, 256], P(('groups', 'pts')), may hold values from -6 to 6
- block_first: int32 [32, 32], replicated, may hold values from 0 to 2, as said below
- block_count: int32 [32, 32], replicated, may hold values from 0 to 2, as said below
Outputs:
- solved_cols: float32 [16384, 256], P(('groups', 'pts'))
- sample_map: float32 [2048, 256], P(('groups', 'pts'))
The draws below stay inside these ranges and needn't reach their ends.
Inputs may be any that keep to these rules, and one draw needn't show every extreme that they name: `block_count`: at most 2; the listed blocks of tile d from source s include every block of s that has a point within distance 1 of some map point of tile d; in every draw some tile owner receives 2 blocks from every source; the totals per owner differ strongly between owners. `block_first`: listed blocks stay inside the source's 4 blocks. `point_pos`: points of one leaf block lie in increasing order within an interval of length 1. `map_pos`: the map points of one tile lie within an interval of length at most 6.
All inputs are finite; a program needn't handle non-finite values.
Results may differ from the reference program's by a relative error of at most 0.003.
Values may be sent and summed in bfloat16 or wider, within the bound.
No kernel may reach another device: no remote copies, remote signals or barrier semaphores. Data moves between devices by JAX's collectives and lax.ppermute only.
A program may use at most 128 MiB of HBM per device.

```python
import jax
import jax.numpy as jnp
from jax import lax

MAP_DEV = 64
SAMPLES = 256
RANK = 128
LEAF = 128
LEVELS = 7
CAP = 2
BLK_DEV = 4
POINTS = 16384
MAPS = 2048
N_PTS = 32


def draw_leaf_inverse(key, part):
    first_key, second_key = jax.random.split(key)
    row_place = jnp.arange(POINTS)[:, None] % LEAF
    column_place = jnp.arange(LEAF)[None, :]
    diagonal = jnp.exp(jax.random.uniform(first_key, (POINTS, LEAF), minval=jnp.log(0.5), maxval=jnp.log(2.0)))
    off_diagonal = jax.random.normal(second_key, (POINTS, LEAF)) * (0.5 / LEAF ** 0.5)
    return jnp.where(row_place == column_place, diagonal, off_diagonal).astype(jnp.float32).astype(jnp.bfloat16)


def draw_basis_right(key, part):
    level_ids = jnp.arange(LEVELS)[:, None, None].astype(jnp.float32)
    half_sizes = POINTS / 2.0 / 2.0 ** level_ids
    base = jax.random.normal(key, (LEVELS, POINTS, RANK))
    return (base / jnp.sqrt(half_sizes)).astype(jnp.float32)


def chord_layout(key):
    offset_key = jax.random.fold_in(key, 21)
    level_key = jax.random.fold_in(key, 22)
    forced_key = jax.random.fold_in(key, 23)
    start_key = jax.random.fold_in(key, 24)
    cell_total = 4 * BLK_DEV
    offsets = jax.random.randint(offset_key, (N_PTS,), 0, 4).astype(jnp.int32)
    level_draw = jax.random.randint(level_key, (N_PTS,), 0, 8)
    widths = jnp.where(level_draw < 5, 1, jnp.where(level_draw < 7, 3, 6)).astype(jnp.int32)
    forced = jax.random.randint(forced_key, (), 0, N_PTS)
    widths = jnp.where(jnp.arange(N_PTS) == forced, 6, widths).astype(jnp.int32)
    starts = jax.random.randint(start_key, (N_PTS,), 1, cell_total - 6).astype(jnp.int32)
    return (offsets, widths, starts)


def table_pair(key):
    offsets, widths, starts = chord_layout(key)
    lower = (starts - 1)[:, None] - offsets[None, :]
    upper = (starts + widths)[:, None] - offsets[None, :]
    first_live = jnp.maximum((lower + 3) // 4, 0)
    last_live = jnp.minimum(upper // 4, BLK_DEV - 1)
    live_total = jnp.maximum(last_live - first_live + 1, 0)
    first = jnp.minimum(first_live, BLK_DEV - CAP)
    count = jnp.where(live_total > 0, last_live - first + 1, 0)
    return (first.astype(jnp.int32), count.astype(jnp.int32))


def draw_block_first(key, part):
    return table_pair(key)[0]


def draw_block_count(key, part):
    return table_pair(key)[1]


def draw_point_pos(key, part):
    offsets, widths, starts = chord_layout(key)
    gap_key = jax.random.fold_in(key, 31)
    gaps = jax.random.uniform(gap_key, (N_PTS, BLK_DEV, LEAF), minval=0.2, maxval=1.0)
    running = jnp.cumsum(gaps, axis=2)
    inside = 0.999 * (running - gaps[:, :, :1]) / running[:, :, -1:]
    cells = (offsets[:, None] + 4 * jnp.arange(BLK_DEV)[None, :]).astype(jnp.float32)
    return (cells[:, :, None] + inside).reshape(POINTS).astype(jnp.float32)


def draw_map_pos(key, part):
    offsets, widths, starts = chord_layout(key)
    spot_key = jax.random.fold_in(key, 32)
    spots = jax.random.uniform(spot_key, (N_PTS, MAP_DEV), minval=0.0, maxval=0.999)
    placed = starts.astype(jnp.float32)[:, None] + widths.astype(jnp.float32)[:, None] * spots
    return placed.reshape(MAPS).astype(jnp.float32)


def level_of(own_key, shape, shards, low, largest):
    level, own = 1.0, jax.random.fold_in(own_key, 6)
    for position, parts in shards:
        steps = jnp.exp(jax.random.uniform(jax.random.fold_in(own, position), (parts,), jnp.float32, low / len(shards), largest / len(shards)))
        level = level * jnp.repeat(steps, shape[position] // parts).reshape([-1 if axis == position else 1 for axis in range(len(shape))])
    return level


def noise(rng, shape, spread, reach, pieces=(), kind=jnp.bfloat16):
    entries = jax.random.normal(rng, shape, jnp.float32) * spread
    if len(pieces) > 0:
        entries = level_of(rng, shape, pieces, -0.22, 0.18) * entries
    return jnp.clip(entries, min=-reach, max=reach).astype(kind)


def setup_inputs(seed: int = 0, part: int = 0) -> dict:
    key_of = jax.random.split(jax.random.key(seed), 10)
    part_splits = jax.random.split(jax.random.fold_in(key_of[9], part), 10)
    return {
        "residual_cols": noise(part_splits[0], (POINTS, SAMPLES), 1.0, 6.0, ((0, 32),)),
        "leaf_inverse": draw_leaf_inverse(jax.random.fold_in(jax.random.fold_in(key_of[9], part), 71), part),
        "basis_left": noise(part_splits[2], (LEVELS, POINTS, RANK), (10 * RANK) ** -0.5, 0.15625, ((1, 32),), jnp.float32),
        "basis_right": draw_basis_right(jax.random.fold_in(jax.random.fold_in(key_of[9], part), 71), part),
        "point_pos": draw_point_pos(jax.random.fold_in(key_of[9], 71), part),
        "map_pos": draw_map_pos(jax.random.fold_in(key_of[9], 71), part),
        "prior_map": noise(part_splits[6], (MAPS, SAMPLES), 1.0, 6.0, ((0, 32),)),
        "block_first": draw_block_first(jax.random.fold_in(key_of[9], 71), part),
        "block_count": draw_block_count(jax.random.fold_in(key_of[9], 71), part),
    }


amplitude = 0.2
highest = lax.Precision.HIGHEST


def wendland(distance):
    scaled = jnp.minimum(jnp.abs(distance) * (2.0 * LEAF), 1.0)
    return (1.0 - scaled) ** 4 * (1.0 + 4.0 * scaled)


def reference(residual_cols, leaf_inverse, basis_left, basis_right, point_pos, map_pos, prior_map, block_first, block_count):
    block_total = POINTS // LEAF
    inverses = leaf_inverse.reshape(block_total, LEAF, LEAF).astype(jnp.float32)
    right_side = residual_cols.reshape(block_total, LEAF, SAMPLES).astype(jnp.float32)
    solved = jnp.einsum("bij,bjs->bis", inverses, right_side, precision=highest).reshape(POINTS, SAMPLES)
    for level_index in reversed(range(LEVELS)):
        half_size = POINTS // 2 ** (level_index + 1)
        node_count = POINTS // (2 * half_size)
        coeff_view = solved.reshape(node_count, 2, half_size, SAMPLES)
        right_view = basis_right[level_index].reshape(node_count, 2, half_size, RANK)
        left_view = basis_left[level_index].reshape(node_count, 2, half_size, RANK)
        projected = jnp.einsum("nhpr,nhps->nhrs", right_view, coeff_view, precision=highest)
        sibling = projected[:, ::-1]
        update = jnp.einsum("nhpr,nhrs->nhps", left_view, sibling, precision=highest)
        solved = solved + update.reshape(POINTS, SAMPLES)
    coeffs = solved.astype(jnp.bfloat16)
    coeff_blocks = coeffs.reshape(N_PTS, BLK_DEV, LEAF, SAMPLES)
    position_blocks = point_pos.reshape(N_PTS, BLK_DEV, LEAF)
    sources = jnp.arange(N_PTS, dtype=jnp.int32)[:, None]
    slot_range = jnp.arange(CAP, dtype=jnp.int32)[None, :]

    def owner_map(owner):
        slot_index = block_first[owner][:, None] + slot_range
        live = slot_range < block_count[owner][:, None]
        data = coeff_blocks[sources, slot_index]
        positions = position_blocks[sources, slot_index]
        targets = lax.dynamic_slice_in_dim(map_pos, owner * MAP_DEV, MAP_DEV)
        kernel = amplitude * wendland(targets[:, None, None, None] - positions[None])
        weights = jnp.where(live[None, :, :, None], kernel, 0.0).astype(jnp.bfloat16)
        return jnp.dot(weights.reshape(MAP_DEV, -1), data.reshape(-1, SAMPLES), preferred_element_type=jnp.float32)

    terms = lax.map(owner_map, jnp.arange(N_PTS, dtype=jnp.int32))
    sample_map = prior_map.astype(jnp.float32) + terms.reshape(MAPS, SAMPLES)
    return solved, sample_map
```

```python
import jax
import jax.numpy as jnp
from jax import lax
from jax.sharding import PartitionSpec as P

CAP = 2
amplitude = 0.2
bf16 = jnp.bfloat16
f32 = jnp.float32
HIGH = lax.Precision.HIGH


def swapped(value, mask):
    pairs = [(source, source ^ mask) for source in range(lax.axis_size("pts"))]
    return lax.ppermute(value, "pts", pairs)


def dot16(a, b):
    return jnp.dot(a.astype(bf16), b.astype(bf16), preferred_element_type=f32)


def halves(value, core):
    width = value.shape[-1] // 2
    low, high = value[..., :width], value[..., width:]
    return jnp.where(core == 0, low, high), jnp.where(core == 0, high, low)


def split3(value):
    one = lax.reduce_precision(value, 8, 7)
    two = lax.reduce_precision(value - one, 8, 7)
    return jnp.concatenate([one, two, value - one - two], 0).astype(bf16)


def body(
    residual_cols,
    leaf_inverse,
    basis_left,
    basis_right,
    point_pos,
    map_pos,
    prior_map,
    block_first,
    block_count,
):
    rows, samples = residual_cols.shape
    leaf = leaf_inverse.shape[1]
    rank = basis_left.shape[2]
    blocks = rows // leaf
    devices = lax.axis_size("pts")
    bits = devices.bit_length() - 1
    me = lax.axis_index("pts")
    core = me % 2
    levels = basis_left.shape[0]
    tile = map_pos.shape[0]
    half = samples // 2

    left16 = basis_left[:bits].astype(bf16)
    right16 = basis_right[:bits].astype(bf16)
    pairs = [(i, j) for j in range(bits) for i in range(j)]
    small = {
        (i, j): lax.dot_general(
            right16[i], left16[j], (((0,), (0,)), ((), ())), preferred_element_type=f32
        )
        for i, j in pairs
    }
    left_other = swapped(left16, 1)

    inverses = leaf_inverse.reshape(blocks, leaf, leaf)
    solved = jnp.einsum(
        "bij,bjs->bis",
        inverses,
        residual_cols.reshape(blocks, leaf, samples),
        preferred_element_type=f32,
    ).reshape(rows, samples)
    for level in reversed(range(bits, levels)):
        size = rows * devices // 2 ** (level + 1)
        nodes = rows // (2 * size)
        view = solved.reshape(nodes, 2, size, samples)
        right = basis_right[level].reshape(nodes, 2, size, rank)
        left = basis_left[level].reshape(nodes, 2, size, rank)
        projected = jnp.einsum("nhpr,nhps->nhrs", right, view, precision=HIGH)
        update = jnp.einsum("nhpr,nhrs->nhps", left, projected[:, ::-1], precision=HIGH)
        solved = solved + update.reshape(rows, samples)
    solved_mine, solved_send = halves(solved, core)
    solved_other = swapped(solved_send, 1)
    projections = jnp.einsum("lpr,ps->lrs", basis_right[:bits], solved, precision=HIGH)
    mine, send = halves(projections, core)

    gathered = map_pos
    shares = [None] * bits
    current = mine
    for bit in range(bits):
        level = bits - 1 - bit
        inner = [(i, j) for i, j in pairs if j <= level]
        outgoing = send if bit == 0 else current
        parts = [outgoing.astype(bf16).reshape(-1, half)]
        parts += [small[p].astype(bf16) for p in inner]
        spots = split3(gathered)
        pad = -spots.size % (16 * half)
        parts.append(jnp.pad(spots, (0, pad)).reshape(-1, half))
        arrived = swapped(jnp.concatenate(parts, 0), 1 << bit)
        theirs = arrived[: (level + 1) * rank].reshape(level + 1, rank, half)
        at = (level + 1) * rank
        small_theirs = {}
        for p in inner:
            small_theirs[p] = arrived[at : at + rank]
            at += rank
        spots = arrived[at:].reshape(-1)[: 3 * gathered.size].reshape(3, -1).astype(f32)
        gathered = jnp.concatenate([gathered, spots[0] + spots[1] + spots[2]], 0)
        shares[level] = theirs[level]
        if level:
            both = jnp.concatenate(
                [
                    jnp.concatenate([small[i, level].astype(bf16) for i in range(level)], 0),
                    jnp.concatenate([small_theirs[i, level] for i in range(level)], 0),
                ],
                1,
            )
            pair = jnp.concatenate([theirs[level], current[level].astype(bf16)], 0)
            step = jnp.dot(both, pair, preferred_element_type=f32).reshape(level, rank, half)
            if bit == 0:
                last_mine = current[level].astype(bf16)
            current = current[:level] + theirs[:level].astype(f32) + step
            small = {
                p: small[p] + small_theirs[p].astype(f32) for p in inner if p[1] < level
            }
        elif bit == 0:
            last_mine = current[level].astype(bf16)

    top = bits - 1
    share = jnp.stack(shares)
    passed = jnp.stack(shares[:top] + [last_mine])
    share_other = swapped(passed, 1)

    def update(left, part):
        return jnp.einsum("lpr,lrs->ps", left, part.astype(left.dtype), precision=HIGH, preferred_element_type=f32)

    final_mine = solved_mine + update(basis_left[:bits], share)
    solved_rest = solved_send + update(basis_left[:bits], share_other)
    final_other = solved_other + update(left_other, passed)
    solved_out = jnp.where(
        core == 0,
        jnp.concatenate([final_mine, solved_rest], 1),
        jnp.concatenate([solved_rest, final_mine], 1),
    )
    coeffs = jnp.concatenate([final_mine, final_other], 0).astype(bf16)

    order = jnp.arange(devices) ^ me
    pick = order[:, None] == jnp.arange(devices)[None, :]
    live = []
    points = []
    for source in (me, me ^ 1):
        first = lax.dynamic_index_in_dim(block_first, source, 1, keepdims=False)
        count = lax.dynamic_index_in_dim(block_count, source, 1, keepdims=False)
        first = jnp.sum(jnp.where(pick, first[None, :], 0), 1)
        count = jnp.sum(jnp.where(pick, count[None, :], 0), 1)
        at = jnp.arange(blocks)[None, :]
        live.append((at >= first[:, None]) & (at < (first + count)[:, None]))
        points.append(lax.dynamic_slice_in_dim(point_pos, source * rows, rows))
    live = jnp.concatenate(live, 1)
    points = jnp.concatenate(points).reshape(2 * blocks, leaf)
    plane = 4
    far = devices // (2 * plane)
    spot_view = gathered.reshape(far, plane, 2 * tile)
    live_view = live.reshape(far, plane, 2, 2 * blocks)
    total = None
    for mask in range(plane):
        spots = spot_view[:, mask].reshape(far, 2, tile)
        r = jnp.minimum(jnp.abs(spots[..., None, None] - points) * (2.0 * leaf), 1.0)
        weight = amplitude * ((1.0 - r) ** 4 * (1.0 + 4.0 * r))
        weight = jnp.where(live_view[:, mask][:, :, None, :, None], weight, 0.0)
        weight = weight.astype(bf16).reshape(far * 2 * tile, 2 * rows)
        partial = jnp.dot(weight, coeffs, preferred_element_type=f32)
        if mask:
            partial = swapped(partial.astype(bf16), mask << 1).astype(f32)
        total = partial if total is None else total + partial
    total = total.reshape(far, 2 * tile, half)
    result = total[0]
    for mask in range(1, far):
        result = result + swapped(total[mask].astype(bf16), mask << 3).astype(f32)
    rest = swapped(result[tile:], 1)
    mapped = jnp.where(
        core == 0,
        jnp.concatenate([result[:tile], rest], 1),
        jnp.concatenate([rest, result[:tile]], 1),
    )
    return (solved_out, prior_map.astype(f32) + mapped)


def solution(mesh):
    in_specs = (
        P(("groups", "pts"), None),
        P(("groups", "pts"), None),
        P(None, ("groups", "pts"), None),
        P(None, ("groups", "pts"), None),
        P(),
        P("pts"),
        P(("groups", "pts"), None),
        P(),
        P(),
    )
    out_specs = (P(("groups", "pts"), None), P(("groups", "pts"), None))
    return jax.shard_map(body, mesh=mesh, in_specs=in_specs, out_specs=out_specs, check_vma=False)
```

```python
import functools

import jax
import jax.numpy as jnp
from jax import lax
from jax.experimental import pallas as pl
from jax.experimental.pallas import tpu as pltpu
from jax.sharding import PartitionSpec as P

CAP = 2
amplitude = 0.2
bf16 = jnp.bfloat16
f32 = jnp.float32
ROOM = 32 * 2**20
VMEM = pl.BlockSpec(memory_space=pltpu.VMEM)
SMEM = pl.BlockSpec(memory_space=pltpu.SMEM)


def swapped(value, mask):
    pairs = [(source, source ^ mask) for source in range(lax.axis_size("pts"))]
    return lax.ppermute(value, "pts", pairs)


def call(kernel, outs, name, flops, moved, ins=None, grid=None, out_specs=None):
    more = {} if grid is None else {"grid": grid, "in_specs": ins, "out_specs": out_specs}
    return pl.pallas_call(
        kernel,
        out_shape=outs,
        name=name,
        compiler_params=pltpu.CompilerParams(vmem_limit_bytes=ROOM),
        cost_estimate=pl.CostEstimate(flops=flops, bytes_accessed=moved, transcendentals=0),
        **more,
    )


def dot(a, b):
    return jnp.dot(a, b, preferred_element_type=f32)


def two(value):
    high = value.astype(bf16)
    return high, (value - high.astype(f32)).astype(bf16)


def dot3(a, b):
    (ah, al), (bh, bl) = a, b
    return dot(ah, bh) + (dot(ah, bl) + dot(al, bh))


def out(shape, kind):
    return jax.ShapeDtypeStruct(shape, kind)


def small_kernel(bits, rank, left_ref, right_ref, small_ref, left16_ref, high_ref, low_ref):
    for i in range(bits):
        high, low = two(right_ref[i].T)
        high_ref[i * rank : (i + 1) * rank, :] = high
        low_ref[i * rank : (i + 1) * rank, :] = low
        left16_ref[i] = left_ref[i].astype(bf16)
    for j in range(1, bits):
        at = j * (j - 1) // 2 * rank
        small_ref[at : at + j * rank, :] = dot(high_ref[: j * rank, :], left16_ref[j]).astype(bf16)


def front_kernel(rows, leaf, sizes, half, core_ref, residual_ref, inverse_ref, high_ref, low_ref, *rest):
    count = 2 * len(sizes)
    bases, (mine_ref, other_ref, keep_ref, send_ref) = rest[:count], rest[count:]
    x = [
        dot(inverse_ref[b * leaf : (b + 1) * leaf, :], residual_ref[b * leaf : (b + 1) * leaf, :])
        for b in range(rows // leaf)
    ]
    x = jnp.concatenate(x, 0)
    for k, size in enumerate(sizes):
        right_ref, left_ref = bases[2 * k], bases[2 * k + 1]
        projected = [
            dot3(two(right_ref[0, a : a + size, :].T), two(x[a : a + size, :]))
            for a in range(0, rows, size)
        ]
        x = jnp.concatenate(
            [
                x[a * size : (a + 1) * size, :]
                + dot3(two(left_ref[0, a * size : (a + 1) * size, :]), two(projected[a ^ 1]))
                for a in range(rows // size)
            ],
            0,
        )
    xh, xl = two(x)
    a = dot(high_ref[...], xh) + (dot(high_ref[...], xl) + dot(low_ref[...], xh))
    first = core_ref[0] == 0
    mine_ref[...] = jnp.where(first, x[:, :half], x[:, half:])
    other_ref[...] = jnp.where(first, x[:, half:], x[:, :half])
    keep_ref[...] = jnp.where(first, a[:, :half], a[:, half:])
    send_ref[...] = jnp.where(first, a[:, half:], a[:, :half]).astype(bf16)


def spread(value, depth):
    value = jnp.concatenate([value, jnp.zeros((depth - value.shape[0], value.shape[1]), f32)], 0) if depth > value.shape[0] else value
    one = value.astype(bf16)
    rest = value - one.astype(f32)
    second = rest.astype(bf16)
    return one, second, (rest - second.astype(f32)).astype(bf16)


def gathered(ref, at, depth):
    a = ref[at : at + depth, :].astype(f32)
    b = ref[at + depth : at + 2 * depth, :].astype(f32)
    return a + b + ref[at + 2 * depth : at + 3 * depth, :].astype(f32)


def put_spots(ref, at, depth, value):
    for k, part in enumerate(spread(value, depth)):
        ref[at + k * depth : at + (k + 1) * depth, :] = part


def linked(level, rank, own, theirs, own_small, their_small):
    cut = level * rank
    mine16, theirs16 = own[cut : cut + rank, :].astype(bf16), theirs[cut : cut + rank, :]
    return own[:cut, :] + theirs[:cut, :].astype(f32) + (dot(own_small, theirs16) + dot(their_small, mine16))


def small_at(level, rank):
    at = level * (level - 1) // 2 * rank
    return slice(at, at + level * rank)


def first_merge(level, rank, depth, keep_ref, got_ref, small_ref, their_ref, spot_ref, y_ref, message_ref, last_ref):
    at = small_at(level, rank)
    y = linked(level, rank, keep_ref[...], got_ref[...], small_ref[at, :], their_ref[at, :])
    y_ref[...] = y
    cut = level * rank
    message_ref[:cut, :] = y.astype(bf16)
    put_spots(message_ref, cut, depth, spot_ref[...])
    last_ref[...] = keep_ref[cut : cut + rank, :].astype(bf16)


def merge(level, rank, apart, counts, depths, y_in, own_ref, got_ref, *rest):
    if apart:
        own_small_ref, their_small_ref, y_ref, message_ref = rest
        base = 0
        spots_at = (level + 1) * rank
    else:
        own_small_ref, their_small_ref = own_ref, got_ref
        y_ref, message_ref = rest
        base = (level + 1) * rank
        spots_at = base + level * (level + 1) // 2 * rank
    at = small_at(level, rank)
    at = slice(base + at.start, base + at.stop)
    y = linked(level, rank, y_in[...], got_ref[...], own_small_ref[at, :], their_small_ref[at, :])
    y_ref[...] = y
    cut = level * rank
    message_ref[:cut, :] = y.astype(bf16)
    inner = level * (level - 1) // 2 * rank
    if inner:
        total = own_small_ref[base : base + inner, :].astype(f32) + their_small_ref[base : base + inner, :].astype(f32)
        message_ref[cut : cut + inner, :] = total.astype(bf16)
    n = counts[0]
    spots = jnp.concatenate(
        [gathered(own_ref, spots_at, depths[0])[:n, :], gathered(got_ref, spots_at, depths[0])[:n, :]], 0
    )
    put_spots(message_ref, cut + inner, depths[1], spots)


def coeff_kernel(bits, rank, mine_ref, other_ref, left_ref, left_other_ref, last_ref, *rest):
    shares, coeff_ref = rest[:bits], rest[bits]
    rows = mine_ref.shape[0]
    for k, (x_ref, l_ref) in enumerate(((mine_ref, left_ref), (other_ref, left_other_ref))):
        x = x_ref[...]
        for level in range(bits):
            share = last_ref if k and level == bits - 1 else shares[level]
            x = x + dot(l_ref[level], share[...])
        coeff_ref[k * rows : (k + 1) * rows, :] = x.astype(bf16)


def weigh_kernel(mask, plane, far, tile, leaf, blocks, n, depth, rank, me_ref, first_ref, count_ref, own_ref, got_ref, point_ref, coeff_ref, out_ref, weight_ref):
    me = me_ref[0]
    scale = 2.0 * leaf
    spots = jnp.concatenate([gathered(own_ref, rank, depth)[:n, :], gathered(got_ref, rank, depth)[:n, :]], 0) * scale
    spots = spots.T
    for z in range(far):
        q = mask + plane * z
        for r in range(2):
            column = jnp.broadcast_to(spots[r * tile : (r + 1) * tile, q : q + 1], (tile, leaf))
            target = me ^ (2 * q + r)
            for b in range(2 * blocks):
                source = me ^ (b // blocks)
                first = first_ref[target, source]
                there = (b % blocks >= first) & (b % blocks < first + count_ref[target, source])
                level = jnp.where(there, amplitude, 0.0)
                distance = jnp.minimum(jnp.abs(column - point_ref[b : b + 1, :] * scale), 1.0)
                left = 1.0 - distance
                left = left * left
                value = (left * left) * (1.0 + 4.0 * distance) * level
                at = (2 * z + r) * tile
                weight_ref[at : at + tile, b * leaf : (b + 1) * leaf] = value.astype(bf16)
    out_ref[...] = dot(weight_ref[...], coeff_ref[...]).astype(out_ref.dtype)


def solved_kernel(bits, core_ref, mine_ref, other_ref, left_ref, *rest):
    shares, others, out_ref = rest[:bits], rest[bits : 2 * bits], rest[2 * bits]
    half = mine_ref.shape[1]
    x, y = mine_ref[...], other_ref[...]
    for level in range(bits):
        high, low = two(left_ref[level])
        a, b = shares[level][...], others[level][...]
        x = x + (dot(high, a) + dot(low, a))
        y = y + (dot(high, b) + dot(low, b))
    first = core_ref[0] == 0
    out_ref[:, :half] = jnp.where(first, x, y)
    out_ref[:, half:] = jnp.where(first, y, x)


def body(
    residual_cols,
    leaf_inverse,
    basis_left,
    basis_right,
    point_pos,
    map_pos,
    prior_map,
    block_first,
    block_count,
):
    rows, samples = residual_cols.shape
    leaf = leaf_inverse.shape[1]
    rank = basis_left.shape[2]
    blocks = rows // leaf
    devices = lax.axis_size("pts")
    bits = devices.bit_length() - 1
    me = lax.axis_index("pts").astype(jnp.int32)
    core = me % 2
    me_s, core_s = me.reshape(1), core.reshape(1)
    levels = basis_left.shape[0]
    tile = map_pos.shape[0]
    half = samples // 2
    pair_count = bits * (bits - 1) // 2

    spot_other = swapped(map_pos, 1)
    top_levels = pl.BlockSpec((bits, rows, rank), lambda g: (0, 0, 0))
    whole = lambda *shape: pl.BlockSpec(shape, lambda g: (0,) * len(shape))
    small, left16, high, low = call(
        functools.partial(small_kernel, bits, rank),
        [
            out((pair_count * rank, rank), bf16),
            out((bits, rows, rank), bf16),
            out((bits * rank, rows), bf16),
            out((bits * rank, rows), bf16),
        ],
        "small",
        2 * pair_count * rank * rank * rows,
        12 * bits * rows * rank,
        ins=[top_levels, top_levels],
        grid=(1,),
        out_specs=[
            whole(pair_count * rank, rank),
            whole(bits, rows, rank),
            whole(bits * rank, rows),
            whole(bits * rank, rows),
        ],
    )(basis_left, basis_right)
    small_other = swapped(small, 1)
    left_other = swapped(left16, 1)

    inner = list(reversed(range(bits, levels)))
    sizes = [rows * devices // 2 ** (level + 1) for level in inner]
    one_level = lambda level: pl.BlockSpec((1, rows, rank), lambda g: (level, 0, 0))
    solved_mine, solved_send, keep, send = call(
        functools.partial(front_kernel, rows, leaf, sizes, half),
        [
            out((rows, half), f32),
            out((rows, half), f32),
            out((bits * rank, half), f32),
            out((bits * rank, half), bf16),
        ],
        "front",
        6 * bits * rank * rows * samples,
        4 * bits * rows * rank,
        ins=[SMEM, whole(rows, samples), whole(rows, leaf), whole(bits * rank, rows), whole(bits * rank, rows)]
        + [one_level(level) for level in inner for _ in range(2)],
        grid=(1,),
        out_specs=[whole(rows, half), whole(rows, half), whole(bits * rank, half), whole(bits * rank, half)],
    )(core_s, residual_cols, leaf_inverse, high, low, *[b for _ in inner for b in (basis_right, basis_left)])
    got = swapped(send, 1)
    solved_other = swapped(solved_send, 1)

    shares, others = [None] * bits, [None] * bits
    top = bits - 1
    depth_of = lambda bit: max(16, 1 << (bit - 1))
    held = top * (top - 1) // 2 * rank
    small_own = (small[:held].astype(f32) + small_other[:held].astype(f32)).astype(bf16)
    small_theirs = swapped(small_own, 2)
    spot_rows = jnp.concatenate([map_pos, spot_other]).reshape(1, 2 * tile)
    y, message, last = call(
        functools.partial(first_merge, top, rank, depth_of(1)),
        [
            out((top * rank, half), f32),
            out((top * rank + 3 * depth_of(1), half), bf16),
            out((rank, half), bf16),
        ],
        "merge0",
        4 * top * rank * rank * half,
        8 * top * rank * half,
    )(keep, got, small, small_other, spot_rows)
    shares[top] = got[top * rank :]
    others[top] = swapped(last, 1)
    for bit in range(1, bits):
        level = top - bit
        arrived = swapped(message, 1 << bit)
        share = arrived[level * rank : (level + 1) * rank]
        shares[level] = share
        others[level] = swapped(share, 1)
        if level:
            inner_rows = level * (level - 1) // 2 * rank
            apart = bit == 1
            y, message = call(
                functools.partial(
                    merge, level, rank, apart, (1 << (bit - 1),), (depth_of(bit), depth_of(bit + 1))
                ),
                [
                    out((level * rank, half), f32),
                    out((level * rank + inner_rows + 3 * depth_of(bit + 1), half), bf16),
                ],
                f"merge{bit}",
                4 * level * rank * rank * half,
                8 * level * rank * half,
            )(y, message, arrived, *((small_own, small_theirs) if apart else ()))

    coeffs = call(
        functools.partial(coeff_kernel, bits, rank),
        out((2 * rows, half), bf16),
        "coeffs",
        4 * bits * rows * rank * half,
        16 * rows * half,
    )(solved_mine, solved_other, left16, left_other, last, *shares)

    points = [lax.dynamic_slice_in_dim(point_pos, s * rows, rows).reshape(blocks, leaf) for s in (me, me ^ 1)]
    points = jnp.concatenate(points, 0)
    plane = 4
    far = devices // (2 * plane)
    depth = depth_of(bits - 1)

    def weighed(mask):
        return pl.pallas_call(
            functools.partial(
                weigh_kernel, mask, plane, far, tile, leaf, blocks, 1 << (bits - 2), depth, rank
            ),
            out_shape=out((far * 2 * tile, half), bf16 if mask else f32),
            in_specs=[SMEM, SMEM, SMEM, VMEM, VMEM, VMEM, VMEM],
            out_specs=VMEM,
            scratch_shapes=[pltpu.VMEM((far * 2 * tile, 2 * rows), bf16)],
            name=f"weigh{mask}",
            compiler_params=pltpu.CompilerParams(vmem_limit_bytes=ROOM),
            cost_estimate=pl.CostEstimate(
                flops=16 * far * tile * rows * half, bytes_accessed=16 * far * tile * half, transcendentals=0
            ),
        )(me_s, block_first, block_count, message, arrived, points, coeffs)

    sent = [swapped(weighed(mask), mask << 1) for mask in (3, 1, 2)]
    total = weighed(0)
    for partial in sent:
        total = total + partial.astype(f32)
    total = total.reshape(far, 2 * tile, half)
    result = total[0]
    for mask in reversed(range(1, far)):
        result = result + swapped(total[mask].astype(bf16), mask << 3).astype(f32)
    rest = swapped(result[tile:], 1)

    solved_out = call(
        functools.partial(solved_kernel, bits),
        out((rows, samples), f32),
        "solved",
        8 * bits * rows * rank * half,
        16 * rows * samples,
        ins=[SMEM, whole(rows, half), whole(rows, half), top_levels] + [whole(rank, half)] * (2 * bits),
        grid=(1,),
        out_specs=whole(rows, samples),
    )(core_s, solved_mine, solved_send, basis_left, *shares, *others)

    mapped = jnp.where(
        core == 0,
        jnp.concatenate([result[:tile], rest], 1),
        jnp.concatenate([rest, result[:tile]], 1),
    )
    return (solved_out, prior_map.astype(f32) + mapped)


def solution(mesh):
    in_specs = (
        P(("groups", "pts"), None),
        P(("groups", "pts"), None),
        P(None, ("groups", "pts"), None),
        P(None, ("groups", "pts"), None),
        P(),
        P("pts"),
        P(("groups", "pts"), None),
        P(),
        P(),
    )
    out_specs = (P(("groups", "pts"), None), P(("groups", "pts"), None))
    return jax.shard_map(body, mesh=mesh, in_specs=in_specs, out_specs=out_specs, check_vma=False)
```

```python
import functools

import jax
import jax.numpy as jnp
from jax import lax
from jax.experimental import pallas as pl
from jax.experimental.pallas import tpu as pltpu
from jax.sharding import PartitionSpec as P

CAP = 2
amplitude = 0.2
bf16 = jnp.bfloat16
f32 = jnp.float32
MIB = 2**20
FRONT = 52
VMEM = pl.BlockSpec(memory_space=pltpu.VMEM)
SMEM = pl.BlockSpec(memory_space=pltpu.SMEM)
HBM = pl.BlockSpec(memory_space=pltpu.HBM)


def swapped(value, mask):
    pairs = [(source, source ^ mask) for source in range(lax.axis_size("pts"))]
    return lax.ppermute(value, "pts", pairs)


def call(kernel, outs, name, flops, moved, room=6, ins=None, scratch=()):
    more = {} if ins is None else {"in_specs": ins}
    return pl.pallas_call(
        kernel,
        out_shape=outs,
        name=name,
        compiler_params=pltpu.CompilerParams(vmem_limit_bytes=room * MIB),
        scratch_shapes=list(scratch),
        cost_estimate=pl.CostEstimate(flops=flops, bytes_accessed=moved, transcendentals=0),
        **more,
    )


def dot(a, b):
    return jnp.dot(a, b, preferred_element_type=f32)


def two(value):
    high = value.astype(bf16)
    return high, (value - high.astype(f32)).astype(bf16)


def dot3(a, b):
    (ah, al), (bh, bl) = a, b
    return dot(ah, bh) + (dot(ah, bl) + dot(al, bh))


def out(shape, kind):
    return jax.ShapeDtypeStruct(shape, kind)


def front_kernel(
    rows, leaf, bits, rank, levels, sizes, half, core_ref, residual_ref, inverse_ref, right_ref, left_ref,
    mine_ref, other_ref, keep_ref, send_ref, small_ref, left16_ref,
    residual_got, inverse_got, right_got, left_got, high_ref, low_ref, sems,
):
    places = [(residual_ref, residual_got), (inverse_ref, inverse_got)]
    order = levels + list(range(bits))
    for level in order:
        places.append((right_ref.at[level], right_got.at[level]))
        places.append((left_ref.at[level], left_got.at[level]))
    copies = [pltpu.make_async_copy(a, b, sems.at[k]) for k, (a, b) in enumerate(places)]
    for copy in copies:
        copy.start()
    right_copy = {level: copies[2 + 2 * k] for k, level in enumerate(order)}
    left_copy = {level: copies[3 + 2 * k] for k, level in enumerate(order)}
    copies[0].wait()
    copies[1].wait()
    x = [
        dot(inverse_got[b * leaf : (b + 1) * leaf, :], residual_got[b * leaf : (b + 1) * leaf, :])
        for b in range(rows // leaf)
    ]
    x = jnp.concatenate(x, 0)
    for level, size in zip(levels, sizes):
        right_copy[level].wait()
        projected = [
            dot3(two(right_got[level, a : a + size, :].T), two(x[a : a + size, :]))
            for a in range(0, rows, size)
        ]
        left_copy[level].wait()
        x = jnp.concatenate(
            [
                x[a * size : (a + 1) * size, :]
                + dot3(two(left_got[level, a * size : (a + 1) * size, :]), two(projected[a ^ 1]))
                for a in range(rows // size)
            ],
            0,
        )
    first = core_ref[0] == 0
    mine_ref[...] = jnp.where(first, x[:, :half], x[:, half:])
    other_ref[...] = jnp.where(first, x[:, half:], x[:, :half])
    xh, xl = two(x)
    for i in range(bits):
        right_copy[i].wait()
        at = slice(i * rank, (i + 1) * rank)
        high, low = two(right_got[i].T)
        high_ref[at, :] = high
        low_ref[at, :] = low
        left_copy[i].wait()
        left16_ref[:, at] = left_got[i].astype(bf16)
        if i:
            small_ref[small_at(i, rank), :] = dot(high_ref[: i * rank, :], left16_ref[:, at]).astype(bf16)
    a = dot(high_ref[...], xh) + (dot(high_ref[...], xl) + dot(low_ref[...], xh))
    keep_ref[...] = jnp.where(first, a[:, :half], a[:, half:])
    send_ref[...] = jnp.where(first, a[:, half:], a[:, :half]).astype(bf16)


def spread(value, depth):
    value = jnp.concatenate([value, jnp.zeros((depth - value.shape[0], value.shape[1]), f32)], 0) if depth > value.shape[0] else value
    one = value.astype(bf16)
    rest = value - one.astype(f32)
    second = rest.astype(bf16)
    return one, second, (rest - second.astype(f32)).astype(bf16)


def gathered(ref, at, depth):
    a = ref[at : at + depth, :].astype(f32)
    b = ref[at + depth : at + 2 * depth, :].astype(f32)
    return a + b + ref[at + 2 * depth : at + 3 * depth, :].astype(f32)


def put_spots(ref, at, depth, value):
    for k, part in enumerate(spread(value, depth)):
        ref[at + k * depth : at + (k + 1) * depth, :] = part


def linked(level, rank, own, theirs, own_small, their_small):
    cut = level * rank
    mine16, theirs16 = own[cut : cut + rank, :].astype(bf16), theirs[cut : cut + rank, :]
    return own[:cut, :] + theirs[:cut, :].astype(f32) + (dot(own_small, theirs16) + dot(their_small, mine16))


def small_at(level, rank):
    at = level * (level - 1) // 2 * rank
    return slice(at, at + level * rank)


def first_merge(level, rank, depth, keep_ref, got_ref, small_ref, their_ref, spot_ref, y_ref, message_ref, last_ref):
    at = small_at(level, rank)
    y = linked(level, rank, keep_ref[...], got_ref[...], small_ref[at, :], their_ref[at, :])
    y_ref[...] = y
    cut = level * rank
    message_ref[:cut, :] = y.astype(bf16)
    put_spots(message_ref, cut, depth, spot_ref[...])
    last_ref[...] = keep_ref[cut : cut + rank, :].astype(bf16)


def merge(level, rank, apart, along, n, depths, y_in, own_ref, got_ref, *rest):
    own_small_ref, their_small_ref = rest[:2] if apart else (own_ref, got_ref)
    y_ref, message_ref = rest[2:] if apart else rest
    base = 0 if apart else (level + 1) * rank
    spots_at = (level + 1) * rank + (0 if apart else level * (level + 1) // 2 * rank)
    at = small_at(level, rank)
    at = slice(base + at.start, base + at.stop)
    y = linked(level, rank, y_in[...], got_ref[...], own_small_ref[at, :], their_small_ref[at, :])
    y_ref[...] = y
    cut = level * rank
    message_ref[:cut, :] = y.astype(bf16)
    inner = level * (level - 1) // 2 * rank if along else 0
    if inner:
        total = own_small_ref[base : base + inner, :].astype(f32) + their_small_ref[base : base + inner, :].astype(f32)
        message_ref[cut : cut + inner, :] = total.astype(bf16)
    spots = jnp.concatenate(
        [gathered(own_ref, spots_at, depths[0])[:n, :], gathered(got_ref, spots_at, depths[0])[:n, :]], 0
    )
    put_spots(message_ref, cut + inner, depths[1], spots)


def partial_kernel(bits, rank, mine_ref, rest_ref, other_ref, left_ref, left_other_ref, last_ref, *refs):
    shares, others, outs = refs[: bits - 1], refs[bits - 1 : 2 * bits - 2], refs[2 * bits - 2 :]
    top = [s[...] for s in shares[:-1]]
    left = left_ref[:, rank:]
    outs[0][...] = mine_ref[...] + dot(left, jnp.concatenate([s[...] for s in shares], 0))
    outs[1][...] = rest_ref[...] + dot(left, jnp.concatenate([s[...] for s in others], 0))
    outs[2][...] = other_ref[...] + dot(left_other_ref[:, rank:], jnp.concatenate(top + [last_ref[...]], 0))


def coeff_kernel(rank, mine_ref, other_ref, left_ref, left_other_ref, got_ref, final_ref, coeff_ref):
    rows = mine_ref.shape[0]
    share = got_ref[:rank, :]
    x = mine_ref[...] + dot(left_ref[:, :rank], share)
    final_ref[...] = x
    coeff_ref[:rows, :] = x.astype(bf16)
    coeff_ref[rows:, :] = (other_ref[...] + dot(left_other_ref[:, :rank], share)).astype(bf16)


def weigh_kernel(mask, plane, far, tile, leaf, blocks, n, depth, rank, me_ref, first_ref, count_ref, own_ref, got_ref, point_ref, coeff_ref, out_ref, weight_ref):
    me = me_ref[0]
    scale = 2.0 * leaf
    spots = jnp.concatenate([gathered(own_ref, rank, depth)[:n, :], gathered(got_ref, rank, depth)[:n, :]], 0) * scale
    spots = spots.T
    weight_ref[...] = jnp.zeros_like(weight_ref)
    for z in range(far):
        q = mask + plane * z
        for r in range(2):
            column = jnp.broadcast_to(spots[r * tile : (r + 1) * tile, q : q + 1], (tile, leaf))
            target = me ^ (2 * q + r)
            at = (2 * z + r) * tile
            for s in range(2):
                first = first_ref[target, me ^ s]
                count = count_ref[target, me ^ s]
                for k in range(CAP):
                    block = s * blocks + first + k
                    level = jnp.where(k < count, amplitude, 0.0)
                    distance = jnp.minimum(jnp.abs(column - point_ref[pl.ds(block, 1), :] * scale), 1.0)
                    left = 1.0 - distance
                    left = left * left
                    value = (left * left) * (1.0 + 4.0 * distance) * level
                    lanes = pl.ds(pl.multiple_of(block * leaf, leaf), leaf)
                    weight_ref[at : at + tile, lanes] = value.astype(bf16)
    out_ref[...] = dot(weight_ref[...], coeff_ref[...]).astype(out_ref.dtype)


def solved_kernel(rank, core_ref, mine_ref, rest_ref, left_ref, share_ref, out_ref):
    half = mine_ref.shape[1]
    x, y = mine_ref[...], rest_ref[...] + dot(left_ref[:, :rank], share_ref[...])
    first = core_ref[0] == 0
    out_ref[:, :half] = jnp.where(first, x, y)
    out_ref[:, half:] = jnp.where(first, y, x)


def body(
    residual_cols,
    leaf_inverse,
    basis_left,
    basis_right,
    point_pos,
    map_pos,
    prior_map,
    block_first,
    block_count,
):
    rows, samples = residual_cols.shape
    leaf = leaf_inverse.shape[1]
    rank = basis_left.shape[2]
    blocks = rows // leaf
    devices = lax.axis_size("pts")
    bits = devices.bit_length() - 1
    me = lax.axis_index("pts").astype(jnp.int32)
    core = me % 2
    me_s, core_s = me.reshape(1), core.reshape(1)
    levels = basis_left.shape[0]
    tile = map_pos.shape[0]
    half = samples // 2
    pair_count = bits * (bits - 1) // 2

    spot_other = swapped(map_pos, 1)
    inner = list(reversed(range(bits, levels)))
    sizes = [rows * devices // 2 ** (level + 1) for level in inner]
    solved_mine, solved_send, keep, send, small, left16 = call(
        functools.partial(front_kernel, rows, leaf, bits, rank, inner, sizes, half),
        [
            out((rows, half), f32),
            out((rows, half), f32),
            out((bits * rank, half), f32),
            out((bits * rank, half), bf16),
            out((pair_count * rank, rank), bf16),
            out((rows, bits * rank), bf16),
        ],
        "front",
        6 * bits * rank * rows * samples,
        8 * levels * rows * rank,
        room=FRONT,
        ins=[SMEM, HBM, HBM, HBM, HBM],
        scratch=[
            pltpu.VMEM((rows, samples), bf16),
            pltpu.VMEM((rows, leaf), bf16),
            pltpu.VMEM((levels, rows, rank), f32),
            pltpu.VMEM((levels, rows, rank), f32),
            pltpu.VMEM((bits * rank, rows), bf16),
            pltpu.VMEM((bits * rank, rows), bf16),
            pltpu.SemaphoreType.DMA((2 + 2 * levels,)),
        ],
    )(core_s, residual_cols, leaf_inverse, basis_right, basis_left)
    small_other = swapped(small, 1)
    left_other = swapped(left16, 1)
    got = swapped(send, 1)
    solved_other = swapped(solved_send, 1)

    shares, others = [None] * bits, [None] * bits
    top = bits - 1
    depth_of = lambda bit: max(16, 1 << (bit - 1))
    pairs_below = lambda level: level * (level - 1) // 2 * rank
    ahead = (1, 2)
    small_own, small_theirs = {}, {}
    previous = small, small_other
    for bit in ahead:
        kept = pairs_below(top - bit + 1)
        small_own[bit] = (previous[0][:kept].astype(f32) + previous[1][:kept].astype(f32)).astype(bf16)
        small_theirs[bit] = swapped(small_own[bit], 1 << bit)
        previous = small_own[bit], small_theirs[bit]
    spot_rows = jnp.concatenate([map_pos, spot_other]).reshape(1, 2 * tile)
    y, message, last = call(
        functools.partial(first_merge, top, rank, depth_of(1)),
        [
            out((top * rank, half), f32),
            out((top * rank + 3 * depth_of(1), half), bf16),
            out((rank, half), bf16),
        ],
        "merge0",
        4 * top * rank * rank * half,
        8 * top * rank * half,
    )(keep, got, small, small_other, spot_rows)
    shares[top] = got[top * rank :]
    others[top] = swapped(last, 1)
    for bit in range(1, bits):
        level = top - bit
        arrived = swapped(message, 1 << bit)
        share = arrived[level * rank : (level + 1) * rank]
        shares[level] = share
        others[level] = swapped(share, 1)
        if level:
            apart, along = bit in ahead, bit + 1 not in ahead
            inner_rows = pairs_below(level) if along else 0
            y, message = call(
                functools.partial(
                    merge, level, rank, apart, along, 1 << (bit - 1), (depth_of(bit), depth_of(bit + 1))
                ),
                [
                    out((level * rank, half), f32),
                    out((level * rank + inner_rows + 3 * depth_of(bit + 1), half), bf16),
                ],
                f"merge{bit}",
                4 * level * rank * rank * half,
                8 * level * rank * half,
            )(y, message, arrived, *((small_own[bit], small_theirs[bit]) if apart else ()))

    part_mine, part_rest, part_other = call(
        functools.partial(partial_kernel, bits, rank),
        [out((rows, half), f32)] * 3,
        "partial",
        6 * bits * rows * rank * half,
        24 * rows * half,
    )(solved_mine, solved_send, solved_other, left16, left_other, last, *shares[1:], *others[1:])
    final_mine, coeffs = call(
        functools.partial(coeff_kernel, rank),
        [out((rows, half), f32), out((2 * rows, half), bf16)],
        "coeffs",
        4 * rows * rank * half,
        16 * rows * half,
    )(part_mine, part_other, left16, left_other, arrived)

    points = [lax.dynamic_slice_in_dim(point_pos, s * rows, rows).reshape(blocks, leaf) for s in (me, me ^ 1)]
    points = jnp.concatenate(points, 0)
    plane = 4
    far = devices // (2 * plane)
    depth = depth_of(bits - 1)

    def weighed(mask, coeffs):
        return call(
            functools.partial(
                weigh_kernel, mask, plane, far, tile, leaf, blocks, 1 << (bits - 2), depth, rank
            ),
            out((far * 2 * tile, half), bf16 if mask else f32),
            f"weigh{mask}",
            16 * far * tile * rows * half,
            16 * far * tile * half,
            room=8 if far <= 4 else 16,
            ins=[SMEM, SMEM, SMEM, VMEM, VMEM, VMEM, VMEM],
            scratch=[pltpu.VMEM((far * 2 * tile, 2 * rows), bf16)],
        )(me_s, block_first, block_count, message, arrived, points, coeffs)

    sent = [swapped(weighed(mask, coeffs), mask << 1) for mask in (3, 1, 2)]
    solved_out = call(
        functools.partial(solved_kernel, rank),
        out((rows, samples), f32),
        "solved",
        2 * rows * rank * half,
        16 * rows * samples,
        ins=[SMEM, VMEM, VMEM, VMEM, VMEM],
    )(core_s, final_mine, part_rest, left16, others[0])
    coeffs, solved_out = lax.optimization_barrier((coeffs, solved_out))
    total = weighed(0, coeffs)
    for partial in sent:
        total = total + partial.astype(f32)
    total = total.reshape(far, 2 * tile, half)
    result = total[0]
    for mask in reversed(range(1, far)):
        result = result + swapped(total[mask].astype(bf16), mask << 3).astype(f32)
    rest = swapped(result[tile:], 1)

    mapped = jnp.where(
        core == 0,
        jnp.concatenate([result[:tile], rest], 1),
        jnp.concatenate([rest, result[:tile]], 1),
    )
    return (solved_out, prior_map.astype(f32) + mapped)


def solution(mesh):
    in_specs = (
        P(("groups", "pts"), None),
        P(("groups", "pts"), None),
        P(None, ("groups", "pts"), None),
        P(None, ("groups", "pts"), None),
        P(),
        P("pts"),
        P(("groups", "pts"), None),
        P(),
        P(),
    )
    out_specs = (P(("groups", "pts"), None), P(("groups", "pts"), None))
    return jax.shard_map(body, mesh=mesh, in_specs=in_specs, out_specs=out_specs, check_vma=False)
```

```python
import functools

import jax
import jax.numpy as jnp
from jax import lax
from jax.experimental import pallas as pl
from jax.experimental.pallas import tpu as pltpu
from jax.sharding import PartitionSpec as P

CAP = 2
amplitude = 0.2
bf16 = jnp.bfloat16
f32 = jnp.float32
MIB = 2**20
FRONT = 52.25
VMEM = pl.BlockSpec(memory_space=pltpu.VMEM)
SMEM = pl.BlockSpec(memory_space=pltpu.SMEM)
HBM = pl.BlockSpec(memory_space=pltpu.HBM)


def swapped(value, mask):
    pairs = [(source, source ^ mask) for source in range(lax.axis_size("pts"))]
    return lax.ppermute(value, "pts", pairs)


def call(kernel, outs, name, flops, moved, room=6, ins=None, scratch=()):
    more = {} if ins is None else {"in_specs": ins}
    return pl.pallas_call(
        kernel,
        out_shape=outs,
        name=name,
        compiler_params=pltpu.CompilerParams(vmem_limit_bytes=int(room * MIB)),
        scratch_shapes=list(scratch),
        cost_estimate=pl.CostEstimate(flops=flops, bytes_accessed=moved, transcendentals=0),
        **more,
    )


def dot(a, b):
    return jnp.dot(a, b, preferred_element_type=f32)


def two(value):
    high = value.astype(bf16)
    return high, (value - high.astype(f32)).astype(bf16)


def dot3(a, b):
    (ah, al), (bh, bl) = a, b
    return dot(ah, bh) + (dot(ah, bl) + dot(al, bh))


def out(shape, kind):
    return jax.ShapeDtypeStruct(shape, kind)


def small_kernel(bits, rank, right_ref, left_ref, small_ref, right_got, left_got, high_ref, sems):
    copies = []
    for i in range(bits - 1):
        copies.append(pltpu.make_async_copy(right_ref.at[i], right_got.at[i], sems.at[2 * i]))
        copies.append(pltpu.make_async_copy(left_ref.at[i + 1], left_got.at[i], sems.at[2 * i + 1]))
    for copy in copies:
        copy.start()
    for i in range(bits - 1):
        copies[2 * i].wait()
        high_ref[i * rank : (i + 1) * rank, :] = right_got[i].astype(bf16).T
        copies[2 * i + 1].wait()
        small_ref[small_at(i + 1, rank), :] = dot(
            high_ref[: (i + 1) * rank, :], left_got[i].astype(bf16)
        ).astype(bf16)


def left_kernel(bits, rank, left_ref, left16_ref, left_got, sems):
    copies = [pltpu.make_async_copy(left_ref.at[i], left_got.at[i], sems.at[i]) for i in range(bits)]
    for copy in copies:
        copy.start()
    for i in range(bits):
        copies[i].wait()
        left16_ref[:, i * rank : (i + 1) * rank] = left_got[i].astype(bf16)


def front_kernel(
    rows, leaf, bits, rank, levels, sizes, half, core_ref, residual_ref, inverse_ref, right_ref, left_ref,
    mine_ref, other_ref, keep_ref, message_ref,
    residual_got, inverse_got, right_got, left_got, high_ref, low_ref, sems,
):
    places = [(residual_ref, residual_got), (inverse_ref, inverse_got)]
    order = levels + list(range(bits))
    for level in order:
        places.append((right_ref.at[level], right_got.at[level]))
    for k, level in enumerate(levels):
        places.append((left_ref.at[level], left_got.at[k]))
    copies = [pltpu.make_async_copy(a, b, sems.at[k]) for k, (a, b) in enumerate(places)]
    for k in (0, 1, *range(2, 2 + len(levels)), *range(2 + len(order), len(places)), *range(2 + len(levels), 2 + len(order))):
        copies[k].start()
    right_copy = {level: copies[2 + k] for k, level in enumerate(order)}
    left_copy = copies[2 + len(order) :]
    copies[0].wait()
    copies[1].wait()
    x = [
        dot(inverse_got[b * leaf : (b + 1) * leaf, :], residual_got[b * leaf : (b + 1) * leaf, :])
        for b in range(rows // leaf)
    ]
    x = jnp.concatenate(x, 0)
    for k, (level, size) in enumerate(zip(levels, sizes)):
        right_copy[level].wait()
        projected = [
            dot3(two(right_got[level, a : a + size, :].T), two(x[a : a + size, :]))
            for a in range(0, rows, size)
        ]
        left_copy[k].wait()
        x = jnp.concatenate(
            [
                x[a * size : (a + 1) * size, :]
                + dot3(two(left_got[k, a * size : (a + 1) * size, :]), two(projected[a ^ 1]))
                for a in range(rows // size)
            ],
            0,
        )
    first = core_ref[0] == 0
    mine_ref[...] = jnp.where(first, x[:, :half], x[:, half:])
    other_ref[...] = jnp.where(first, x[:, half:], x[:, :half])
    xh, xl = two(x)
    for i in range(bits):
        right_copy[i].wait()
        at = slice(i * rank, (i + 1) * rank)
        high, low = two(right_got[i].T)
        high_ref[at, :] = high
        low_ref[at, :] = low
    a = dot(high_ref[...], xh) + (dot(high_ref[...], xl) + dot(low_ref[...], xh))
    keep_ref[...] = jnp.where(first, a[:, :half], a[:, half:])
    message_ref[...] = jnp.where(first, a[:, half:], a[:, :half]).astype(bf16)


def spread(value, depth):
    value = jnp.concatenate([value, jnp.zeros((depth - value.shape[0], value.shape[1]), f32)], 0) if depth > value.shape[0] else value
    one = value.astype(bf16)
    rest = value - one.astype(f32)
    second = rest.astype(bf16)
    return one, second, (rest - second.astype(f32)).astype(bf16)


def gathered(ref, at, depth):
    a = ref[at : at + depth, :].astype(f32)
    b = ref[at + depth : at + 2 * depth, :].astype(f32)
    return a + b + ref[at + 2 * depth : at + 3 * depth, :].astype(f32)


def put_spots(ref, at, depth, value):
    for k, part in enumerate(spread(value, depth)):
        ref[at + k * depth : at + (k + 1) * depth, :] = part


def linked(level, rank, own, theirs, own_small, their_small):
    cut = level * rank
    mine16, theirs16 = own[cut : cut + rank, :].astype(bf16), theirs[cut : cut + rank, :]
    return own[:cut, :] + theirs[:cut, :].astype(f32) + (dot(own_small, theirs16) + dot(their_small, mine16))


def small_at(level, rank):
    at = level * (level - 1) // 2 * rank
    return slice(at, at + level * rank)


def first_merge(level, rank, depth, keep_ref, got_ref, small_ref, their_ref, spot_ref, y_ref, message_ref, last_ref):
    at = small_at(level, rank)
    y = linked(level, rank, keep_ref[...], got_ref[...], small_ref[at, :], their_ref[at, :])
    y_ref[...] = y
    cut = level * rank
    message_ref[:cut, :] = y.astype(bf16)
    put_spots(message_ref, cut, depth, spot_ref[...])
    last_ref[...] = keep_ref[cut : cut + rank, :].astype(bf16)


def merge(level, rank, apart, along, n, depths, y_in, own_ref, got_ref, *rest):
    own_small_ref, their_small_ref = rest[:2] if apart else (own_ref, got_ref)
    *y_ref, message_ref = rest[2:] if apart else rest
    base = 0 if apart else (level + 1) * rank
    spots_at = (level + 1) * rank + (0 if apart else level * (level + 1) // 2 * rank)
    at = small_at(level, rank)
    at = slice(base + at.start, base + at.stop)
    y = linked(level, rank, y_in[...], got_ref[...], own_small_ref[at, :], their_small_ref[at, :])
    if y_ref:
        y_ref[0][...] = y
    cut = level * rank
    message_ref[:cut, :] = y.astype(bf16)
    inner = level * (level - 1) // 2 * rank if along else 0
    if inner:
        total = own_small_ref[base : base + inner, :].astype(f32) + their_small_ref[base : base + inner, :].astype(f32)
        message_ref[cut : cut + inner, :] = total.astype(bf16)
    spots = jnp.concatenate(
        [gathered(own_ref, spots_at, depths[0])[:n, :], gathered(got_ref, spots_at, depths[0])[:n, :]], 0
    )
    put_spots(message_ref, cut + inner, depths[1], spots)


def partial_kernel(bits, rank, mine_ref, rest_ref, other_ref, left_ref, left_other_ref, last_ref, *refs):
    shares, others, outs = refs[: bits - 1], refs[bits - 1 : 2 * bits - 2], refs[2 * bits - 2 :]
    top = [s[...] for s in shares[:-1]]
    left = left_ref[:, rank:]
    outs[0][...] = mine_ref[...] + dot(left, jnp.concatenate([s[...] for s in shares], 0))
    outs[1][...] = rest_ref[...] + dot(left, jnp.concatenate([s[...] for s in others], 0))
    outs[2][...] = other_ref[...] + dot(left_other_ref[:, rank:], jnp.concatenate(top + [last_ref[...]], 0))


def coeff_kernel(rank, n, depth, scale, mine_ref, other_ref, left_ref, left_other_ref, got_ref, final_ref, coeff_ref, spot_ref):
    rows = mine_ref.shape[0]
    share = got_ref[:rank, :]
    x = mine_ref[...] + dot(left_ref[:, :rank], share)
    final_ref[...] = x
    coeff_ref[:rows, :] = x.astype(bf16)
    coeff_ref[rows:, :] = (other_ref[...] + dot(left_other_ref[:, :rank], share)).astype(bf16)
    spot_ref[...] = (gathered(got_ref, rank, depth)[:n, :] * scale).T


def weigh(tile, leaf, blocks, devices, info_ref, spots, point_ref, weight_ref, q, column_at, at):
    scale = 2.0 * leaf
    for r in range(2):
        column = jnp.broadcast_to(spots[r * tile : (r + 1) * tile, column_at : column_at + 1], (tile, leaf))
        target = info_ref[0] ^ (2 * q + r)
        for s in range(2):
            first = info_ref[1 + s * devices + target]
            count = info_ref[1 + (2 + s) * devices + target]
            for k in range(CAP):
                block = s * blocks + first + k
                level = jnp.where(k < count, amplitude, 0.0)
                distance = jnp.minimum(jnp.abs(column - point_ref[pl.ds(block, 1), :] * scale), 1.0)
                left = 1.0 - distance
                left = left * left
                value = (left * left) * (1.0 + 4.0 * distance) * level
                lanes = pl.ds(pl.multiple_of(block * leaf, leaf), leaf)
                weight_ref[at + r * tile : at + (r + 1) * tile, lanes] = value.astype(bf16)


def near_kernel(plane, near, tile, leaf, blocks, devices, n, depth, rank, info_ref, own_ref, point_ref, *weight_refs):
    spots = (gathered(own_ref, rank, depth)[:n, :] * (2.0 * leaf)).T
    for mask in range(plane):
        weight_refs[mask][...] = jnp.zeros_like(weight_refs[mask])
        for z in range(near):
            q = mask + plane * z
            weigh(tile, leaf, blocks, devices, info_ref, spots, point_ref, weight_refs[mask], q, q, 2 * z * tile)


def far_kernel(mask, plane, near, tile, leaf, blocks, devices, info_ref, spot_ref, near_ref, point_ref, coeff_ref, out_ref, weight_ref):
    spots = spot_ref[...]
    weight_ref[...] = jnp.zeros_like(weight_ref)
    for z in range(near):
        column = mask + plane * z
        weigh(
            tile, leaf, blocks, devices, info_ref, spots, point_ref, weight_ref,
            column + plane * near, column, 2 * z * tile,
        )
    half = 2 * near * tile
    out_ref[:half, :] = dot(near_ref[...], coeff_ref[...]).astype(out_ref.dtype)
    out_ref[half:, :] = dot(weight_ref[...], coeff_ref[...]).astype(out_ref.dtype)


def solved_kernel(rank, core_ref, mine_ref, rest_ref, left_ref, share_ref, out_ref):
    half = mine_ref.shape[1]
    x, y = mine_ref[...], rest_ref[...] + dot(left_ref[:, :rank], share_ref[...])
    first = core_ref[0] == 0
    out_ref[:, :half] = jnp.where(first, x, y)
    out_ref[:, half:] = jnp.where(first, y, x)


def body(
    residual_cols,
    leaf_inverse,
    basis_left,
    basis_right,
    point_pos,
    map_pos,
    prior_map,
    block_first,
    block_count,
):
    rows, samples = residual_cols.shape
    leaf = leaf_inverse.shape[1]
    rank = basis_left.shape[2]
    blocks = rows // leaf
    devices = lax.axis_size("pts")
    bits = devices.bit_length() - 1
    me = lax.axis_index("pts").astype(jnp.int32)
    core = me % 2
    core_s = core.reshape(1)
    levels = basis_left.shape[0]
    tile = map_pos.shape[0]
    half = samples // 2
    pair_count = bits * (bits - 1) // 2

    spot_other = swapped(map_pos, 1)
    inner = list(reversed(range(bits, levels)))
    sizes = [rows * devices // 2 ** (level + 1) for level in inner]
    small = call(
        functools.partial(small_kernel, bits, rank),
        out((pair_count * rank, rank), bf16),
        "small",
        2 * pair_count * rank * rank * rows,
        8 * bits * rows * rank,
        room=FRONT,
        ins=[HBM, HBM],
        scratch=[
            pltpu.VMEM((bits - 1, rows, rank), f32),
            pltpu.VMEM((bits - 1, rows, rank), f32),
            pltpu.VMEM(((bits - 1) * rank, rows), bf16),
            pltpu.SemaphoreType.DMA((2 * bits - 2,)),
        ],
    )(basis_right, basis_left)
    small_other = swapped(small, 1)
    solved_mine, solved_send, keep, send = call(
        functools.partial(front_kernel, rows, leaf, bits, rank, inner, sizes, half),
        [
            out((rows, half), f32),
            out((rows, half), f32),
            out((bits * rank, half), f32),
            out((bits * rank, half), bf16),
        ],
        "front",
        6 * bits * rank * rows * samples,
        8 * levels * rows * rank,
        room=FRONT,
        ins=[SMEM, HBM, HBM, HBM, HBM],
        scratch=[
            pltpu.VMEM((rows, samples), bf16),
            pltpu.VMEM((rows, leaf), bf16),
            pltpu.VMEM((levels, rows, rank), f32),
            pltpu.VMEM((max(1, len(inner)), rows, rank), f32),
            pltpu.VMEM((bits * rank, rows), bf16),
            pltpu.VMEM((bits * rank, rows), bf16),
            pltpu.SemaphoreType.DMA((2 + levels + max(1, len(inner)),)),
        ],
    )(core_s, residual_cols, leaf_inverse, basis_right, basis_left)
    got = swapped(send, 1)
    solved_other = swapped(solved_send, 1)
    left16 = call(
        functools.partial(left_kernel, bits, rank),
        out((rows, bits * rank), bf16),
        "left16",
        bits * rows * rank,
        6 * bits * rows * rank,
        room=24,
        ins=[HBM],
        scratch=[pltpu.VMEM((bits, rows, rank), f32), pltpu.SemaphoreType.DMA((bits,))],
    )(basis_left)
    left_other = swapped(left16, 1)

    shares, others = [None] * bits, [None] * bits
    top = bits - 1
    depth_of = lambda bit: max(16, 1 << (bit - 1))
    pairs_below = lambda level: level * (level - 1) // 2 * rank
    spot_rows = jnp.concatenate([map_pos, spot_other]).reshape(1, 2 * tile)
    y, message, last = call(
        functools.partial(first_merge, top, rank, depth_of(1)),
        [
            out((top * rank, half), f32),
            out((top * rank + 3 * depth_of(1), half), bf16),
            out((rank, half), bf16),
        ],
        "merge0",
        4 * top * rank * rank * half,
        8 * top * rank * half,
    )(keep, got, small, small_other, spot_rows)
    ahead = (1, 2)
    small_own, small_theirs = {}, {}
    previous = small, small_other
    for bit in ahead:
        kept = pairs_below(top - bit + 1)
        both = (previous[0][:kept].astype(f32) + previous[1][:kept].astype(f32)).astype(bf16)
        small_own[bit] = both
        small_theirs[bit] = swapped(both, 1 << bit)
        previous = small_own[bit], small_theirs[bit]
    shares[top] = got[top * rank :]
    others[top] = swapped(last, 1)
    for bit in range(1, bits):
        level = top - bit
        arrived = swapped(message, 1 << bit)
        share = arrived[level * rank : (level + 1) * rank]
        shares[level] = share
        others[level] = swapped(share, 1)
        if level:
            apart, along = bit in ahead, bit + 1 not in ahead
            inner_rows = pairs_below(level) if along else 0
            *kept_y, message = call(
                functools.partial(
                    merge, level, rank, apart, along, 1 << (bit - 1), (depth_of(bit), depth_of(bit + 1))
                ),
                [out((level * rank, half), f32)] * (level > 1)
                + [out((level * rank + inner_rows + 3 * depth_of(bit + 1), half), bf16)],
                f"merge{bit}",
                4 * level * rank * rank * half,
                8 * level * rank * half,
            )(y, message, arrived, *((small_own[bit], small_theirs[bit]) if apart else ()))
            y = kept_y[0] if kept_y else None

    part_mine, part_rest, part_other = call(
        functools.partial(partial_kernel, bits, rank),
        [out((rows, half), f32)] * 3,
        "partial",
        6 * bits * rows * rank * half,
        24 * rows * half,
    )(solved_mine, solved_send, solved_other, left16, left_other, last, *shares[1:], *others[1:])
    plane = 4
    near = devices // (4 * plane)
    depth = depth_of(bits - 1)
    chips = 1 << (bits - 2)
    points = [lax.dynamic_slice_in_dim(point_pos, s * rows, rows).reshape(blocks, leaf) for s in (me, me ^ 1)]
    points = jnp.concatenate(points, 0)
    info = jnp.concatenate(
        [me.reshape(1)]
        + [lax.dynamic_index_in_dim(t, s, 1, keepdims=False) for t in (block_first, block_count) for s in (me, me ^ 1)]
    )
    near_weights = call(
        functools.partial(near_kernel, plane, near, tile, leaf, blocks, devices, chips, depth, rank),
        [out((2 * near * tile, 2 * rows), bf16)] * plane,
        "near",
        40 * plane * near * tile * rows,
        8 * plane * near * tile * rows,
        room=8 if near <= 4 else 24,
        ins=[SMEM, VMEM, VMEM],
    )(info, message, points)
    final_mine, coeffs, spots = call(
        functools.partial(coeff_kernel, rank, chips, depth, 2.0 * leaf),
        [out((rows, half), f32), out((2 * rows, half), bf16), out((2 * tile, chips), f32)],
        "coeffs",
        4 * rows * rank * half,
        16 * rows * half,
    )(part_mine, part_other, left16, left_other, arrived)

    def weighed(mask, coeffs):
        return call(
            functools.partial(far_kernel, mask, plane, near, tile, leaf, blocks, devices),
            out((4 * near * tile, half), bf16 if mask else f32),
            f"weigh{mask}",
            32 * near * tile * rows * half,
            32 * near * tile * half,
            room=8 if near <= 4 else 16,
            ins=[SMEM, VMEM, VMEM, VMEM, VMEM],
            scratch=[pltpu.VMEM((2 * near * tile, 2 * rows), bf16)],
        )(info, spots, near_weights[mask], points, coeffs)

    sent = []
    for mask in (3, 2, 1):
        if mask == 1:
            coeffs, others[0] = lax.optimization_barrier((coeffs, others[0]))
        partial = weighed(mask, coeffs)
        coeffs, partial = lax.optimization_barrier((coeffs, partial))
        sent.append(swapped(partial, mask << 1))
    solved_out = call(
        functools.partial(solved_kernel, rank),
        out((rows, samples), f32),
        "solved",
        2 * rows * rank * half,
        16 * rows * samples,
        ins=[SMEM, VMEM, VMEM, VMEM, VMEM],
    )(core_s, final_mine, part_rest, left16, others[0])
    coeffs, solved_out = lax.optimization_barrier((coeffs, solved_out))
    total = weighed(0, coeffs)
    for partial in sent:
        total = total + partial.astype(f32)
    far = 2 * near
    total = total.reshape(far, 2 * tile, half)
    result = total[0]
    for mask in range(1, far):
        result = result + swapped(total[mask].astype(bf16), mask << 3).astype(f32)
    rest = swapped(result[tile:], 1)

    mapped = jnp.where(
        core == 0,
        jnp.concatenate([result[:tile], rest], 1),
        jnp.concatenate([rest, result[:tile]], 1),
    )
    return (solved_out, prior_map.astype(f32) + mapped)


def solution(mesh):
    in_specs = (
        P(("groups", "pts"), None),
        P(("groups", "pts"), None),
        P(None, ("groups", "pts"), None),
        P(None, ("groups", "pts"), None),
        P(),
        P("pts"),
        P(("groups", "pts"), None),
        P(),
        P(),
    )
    out_specs = (P(("groups", "pts"), None), P(("groups", "pts"), None))
    return jax.shard_map(body, mesh=mesh, in_specs=in_specs, out_specs=out_specs, check_vma=False)
```

```python
import functools

import jax
import jax.numpy as jnp
from jax import lax
from jax.experimental import pallas as pl
from jax.experimental.pallas import tpu as pltpu
from jax.sharding import PartitionSpec as P

CAP = 2
amplitude = 0.2
bf16 = jnp.bfloat16
f32 = jnp.float32
MIB = 2**20
FRONT = 52.25
VMEM = pl.BlockSpec(memory_space=pltpu.VMEM)
SMEM = pl.BlockSpec(memory_space=pltpu.SMEM)
HBM = pl.BlockSpec(memory_space=pltpu.HBM)


def swapped(value, mask):
    pairs = [(source, source ^ mask) for source in range(lax.axis_size("pts"))]
    return lax.ppermute(value, "pts", pairs)


def call(kernel, outs, name, flops, moved, room=6, ins=None, scratch=()):
    more = {} if ins is None else {"in_specs": ins}
    return pl.pallas_call(
        kernel,
        out_shape=outs,
        name=name,
        compiler_params=pltpu.CompilerParams(vmem_limit_bytes=int(room * MIB)),
        scratch_shapes=list(scratch),
        cost_estimate=pl.CostEstimate(flops=flops, bytes_accessed=moved, transcendentals=0),
        **more,
    )


def dot(a, b):
    return jnp.dot(a, b, preferred_element_type=f32)


def two(value):
    high = value.astype(bf16)
    return high, (value - high.astype(f32)).astype(bf16)


def dot3(a, b):
    (ah, al), (bh, bl) = a, b
    return dot(ah, bh) + (dot(ah, bl) + dot(al, bh))


def out(shape, kind):
    return jax.ShapeDtypeStruct(shape, kind)


def small_kernel(bits, rank, right_ref, left_ref, small_ref, right_got, left_got, high_ref, sems):
    copies = []
    for i in range(bits - 1):
        copies.append(pltpu.make_async_copy(right_ref.at[i], right_got.at[i], sems.at[2 * i]))
        copies.append(pltpu.make_async_copy(left_ref.at[i + 1], left_got.at[i], sems.at[2 * i + 1]))
    for copy in copies:
        copy.start()
    for i in range(bits - 1):
        copies[2 * i].wait()
        high_ref[i * rank : (i + 1) * rank, :] = right_got[i].astype(bf16).T
        copies[2 * i + 1].wait()
        small_ref[small_at(i + 1, rank), :] = dot(
            high_ref[: (i + 1) * rank, :], left_got[i].astype(bf16)
        ).astype(bf16)


def left_kernel(bits, rank, left_ref, left16_ref, left_got, sems):
    copies = [pltpu.make_async_copy(left_ref.at[i], left_got.at[i], sems.at[i]) for i in range(bits)]
    for copy in copies:
        copy.start()
    for i in range(bits):
        copies[i].wait()
        left16_ref[:, i * rank : (i + 1) * rank] = left_got[i].astype(bf16)


def front_kernel(
    rows, leaf, bits, rank, levels, sizes, half, core_ref, residual_ref, inverse_ref, right_ref, left_ref,
    mine_ref, other_ref, keep_ref, message_ref,
    residual_got, inverse_got, right_got, left_got, high_ref, low_ref, sems,
):
    places = [(residual_ref, residual_got), (inverse_ref, inverse_got)]
    order = levels + list(range(bits))
    for level in order:
        places.append((right_ref.at[level], right_got.at[level]))
    for k, level in enumerate(levels):
        places.append((left_ref.at[level], left_got.at[k]))
    copies = [pltpu.make_async_copy(a, b, sems.at[k]) for k, (a, b) in enumerate(places)]
    for k in (0, 1, *range(2, 2 + len(levels)), *range(2 + len(order), len(places)), *range(2 + len(levels), 2 + len(order))):
        copies[k].start()
    right_copy = {level: copies[2 + k] for k, level in enumerate(order)}
    left_copy = copies[2 + len(order) :]
    copies[0].wait()
    copies[1].wait()
    x = [
        dot(inverse_got[b * leaf : (b + 1) * leaf, :], residual_got[b * leaf : (b + 1) * leaf, :])
        for b in range(rows // leaf)
    ]
    x = jnp.concatenate(x, 0)
    for k, (level, size) in enumerate(zip(levels, sizes)):
        right_copy[level].wait()
        projected = [
            dot3(two(right_got[level, a : a + size, :].T), two(x[a : a + size, :]))
            for a in range(0, rows, size)
        ]
        left_copy[k].wait()
        x = jnp.concatenate(
            [
                x[a * size : (a + 1) * size, :]
                + dot3(two(left_got[k, a * size : (a + 1) * size, :]), two(projected[a ^ 1]))
                for a in range(rows // size)
            ],
            0,
        )
    first = core_ref[0] == 0
    mine_ref[...] = jnp.where(first, x[:, :half], x[:, half:])
    other_ref[...] = jnp.where(first, x[:, half:], x[:, :half])
    xh, xl = two(x)
    for i in range(bits):
        right_copy[i].wait()
        at = slice(i * rank, (i + 1) * rank)
        high, low = two(right_got[i].T)
        high_ref[at, :] = high
        low_ref[at, :] = low
    a = dot(high_ref[...], xh) + (dot(high_ref[...], xl) + dot(low_ref[...], xh))
    keep_ref[...] = jnp.where(first, a[:, :half], a[:, half:])
    message_ref[...] = jnp.where(first, a[:, half:], a[:, :half]).astype(bf16)


def spread(value, depth):
    value = jnp.concatenate([value, jnp.zeros((depth - value.shape[0], value.shape[1]), f32)], 0) if depth > value.shape[0] else value
    one = value.astype(bf16)
    rest = value - one.astype(f32)
    second = rest.astype(bf16)
    return one, second, (rest - second.astype(f32)).astype(bf16)


def gathered(ref, at, depth):
    a = ref[at : at + depth, :].astype(f32)
    b = ref[at + depth : at + 2 * depth, :].astype(f32)
    return a + b + ref[at + 2 * depth : at + 3 * depth, :].astype(f32)


def put_spots(ref, at, depth, value):
    for k, part in enumerate(spread(value, depth)):
        ref[at + k * depth : at + (k + 1) * depth, :] = part


def linked(level, rank, own, theirs, own_small, their_small):
    cut = level * rank
    mine16, theirs16 = own[cut : cut + rank, :].astype(bf16), theirs[cut : cut + rank, :]
    return own[:cut, :] + theirs[:cut, :].astype(f32) + (dot(own_small, theirs16) + dot(their_small, mine16))


def small_at(level, rank):
    at = level * (level - 1) // 2 * rank
    return slice(at, at + level * rank)


def first_merge(level, rank, depth, keep_ref, got_ref, small_ref, their_ref, spot_ref, y_ref, message_ref, last_ref):
    at = small_at(level, rank)
    y = linked(level, rank, keep_ref[...], got_ref[...], small_ref[at, :], their_ref[at, :])
    y_ref[...] = y
    cut = level * rank
    message_ref[:cut, :] = y.astype(bf16)
    put_spots(message_ref, cut, depth, spot_ref[...])
    last_ref[...] = keep_ref[cut : cut + rank, :].astype(bf16)


def merge(level, rank, apart, along, n, depths, y_in, own_ref, got_ref, *rest):
    own_small_ref, their_small_ref = rest[:2] if apart else (own_ref, got_ref)
    *y_ref, message_ref = rest[2:] if apart else rest
    base = 0 if apart else (level + 1) * rank
    spots_at = (level + 1) * rank + (0 if apart else level * (level + 1) // 2 * rank)
    at = small_at(level, rank)
    at = slice(base + at.start, base + at.stop)
    y = linked(level, rank, y_in[...], got_ref[...], own_small_ref[at, :], their_small_ref[at, :])
    if y_ref:
        y_ref[0][...] = y
    cut = level * rank
    message_ref[:cut, :] = y.astype(bf16)
    inner = level * (level - 1) // 2 * rank if along else 0
    if inner:
        total = own_small_ref[base : base + inner, :].astype(f32) + their_small_ref[base : base + inner, :].astype(f32)
        message_ref[cut : cut + inner, :] = total.astype(bf16)
    spots = jnp.concatenate(
        [gathered(own_ref, spots_at, depths[0])[:n, :], gathered(got_ref, spots_at, depths[0])[:n, :]], 0
    )
    put_spots(message_ref, cut + inner, depths[1], spots)


def partial_kernel(bits, rank, mine_ref, other_ref, left_ref, left_other_ref, last_ref, *refs):
    shares, outs = refs[: bits - 2], refs[bits - 2 :]
    top = [s[...] for s in shares[:-1]]
    outs[0][...] = mine_ref[...] + dot(left_ref[:, 2 * rank :], jnp.concatenate([s[...] for s in shares], 0))
    outs[1][...] = other_ref[...] + dot(left_other_ref[:, 2 * rank :], jnp.concatenate(top + [last_ref[...]], 0))


def coeff_kernel(rank, n, depth, scale, mine_ref, other_ref, left_ref, left_other_ref, share_ref, got_ref, final_ref, coeff_ref, spot_ref):
    rows = mine_ref.shape[0]
    share = jnp.concatenate([got_ref[:rank, :], share_ref[...]], 0)
    x = mine_ref[...] + dot(left_ref[:, : 2 * rank], share)
    final_ref[...] = x
    coeff_ref[:rows, :] = x.astype(bf16)
    coeff_ref[rows:, :] = (other_ref[...] + dot(left_other_ref[:, : 2 * rank], share)).astype(bf16)
    spot_ref[...] = (gathered(got_ref, rank, depth)[:n, :] * scale).T


def weigh(tile, leaf, blocks, devices, info_ref, spots, point_ref, weight_ref, q, column_at, at):
    scale = 2.0 * leaf
    for r in range(2):
        column = jnp.broadcast_to(spots[r * tile : (r + 1) * tile, column_at : column_at + 1], (tile, leaf))
        target = info_ref[0] ^ (2 * q + r)
        for s in range(2):
            first = info_ref[1 + s * devices + target]
            count = info_ref[1 + (2 + s) * devices + target]
            for k in range(CAP):
                block = s * blocks + first + k
                level = jnp.where(k < count, amplitude, 0.0)
                distance = jnp.minimum(jnp.abs(column - point_ref[pl.ds(block, 1), :] * scale), 1.0)
                left = 1.0 - distance
                left = left * left
                value = (left * left) * (1.0 + 4.0 * distance) * level
                lanes = pl.ds(pl.multiple_of(block * leaf, leaf), leaf)
                weight_ref[at + r * tile : at + (r + 1) * tile, lanes] = value.astype(bf16)


def near_kernel(plane, near, tile, leaf, blocks, devices, n, depth, rank, info_ref, own_ref, point_ref, *weight_refs):
    spots = (gathered(own_ref, rank, depth)[:n, :] * (2.0 * leaf)).T
    for mask in range(plane):
        weight_refs[mask][...] = jnp.zeros_like(weight_refs[mask])
        for z in range(near):
            q = mask + plane * z
            weigh(tile, leaf, blocks, devices, info_ref, spots, point_ref, weight_refs[mask], q, q, 2 * z * tile)


def far_kernel(mask, plane, near, tile, leaf, blocks, devices, info_ref, spot_ref, near_ref, point_ref, coeff_ref, out_ref, weight_ref):
    spots = spot_ref[...]
    weight_ref[...] = jnp.zeros_like(weight_ref)
    for z in range(near):
        column = mask + plane * z
        weigh(
            tile, leaf, blocks, devices, info_ref, spots, point_ref, weight_ref,
            column + plane * near, column, 2 * z * tile,
        )
    half = 2 * near * tile
    out_ref[:half, :] = dot(near_ref[...], coeff_ref[...]).astype(out_ref.dtype)
    out_ref[half:, :] = dot(weight_ref[...], coeff_ref[...]).astype(out_ref.dtype)


def solved_kernel(core_ref, mine_ref, rest_ref, left_ref, *refs):
    others, out_ref = refs[:-1], refs[-1]
    half = mine_ref.shape[1]
    x, y = mine_ref[...], rest_ref[...] + dot(left_ref[...], jnp.concatenate([s[...] for s in others], 0))
    first = core_ref[0] == 0
    out_ref[:, :half] = jnp.where(first, x, y)
    out_ref[:, half:] = jnp.where(first, y, x)


def body(
    residual_cols,
    leaf_inverse,
    basis_left,
    basis_right,
    point_pos,
    map_pos,
    prior_map,
    block_first,
    block_count,
):
    rows, samples = residual_cols.shape
    leaf = leaf_inverse.shape[1]
    rank = basis_left.shape[2]
    blocks = rows // leaf
    devices = lax.axis_size("pts")
    bits = devices.bit_length() - 1
    me = lax.axis_index("pts").astype(jnp.int32)
    core = me % 2
    core_s = core.reshape(1)
    levels = basis_left.shape[0]
    tile = map_pos.shape[0]
    half = samples // 2
    pair_count = bits * (bits - 1) // 2

    spot_other = swapped(map_pos, 1)
    inner = list(reversed(range(bits, levels)))
    sizes = [rows * devices // 2 ** (level + 1) for level in inner]
    small = call(
        functools.partial(small_kernel, bits, rank),
        out((pair_count * rank, rank), bf16),
        "small",
        2 * pair_count * rank * rank * rows,
        8 * bits * rows * rank,
        room=FRONT,
        ins=[HBM, HBM],
        scratch=[
            pltpu.VMEM((bits - 1, rows, rank), f32),
            pltpu.VMEM((bits - 1, rows, rank), f32),
            pltpu.VMEM(((bits - 1) * rank, rows), bf16),
            pltpu.SemaphoreType.DMA((2 * bits - 2,)),
        ],
    )(basis_right, basis_left)
    small_other = swapped(small, 1)
    solved_mine, solved_send, keep, send = call(
        functools.partial(front_kernel, rows, leaf, bits, rank, inner, sizes, half),
        [
            out((rows, half), f32),
            out((rows, half), f32),
            out((bits * rank, half), f32),
            out((bits * rank, half), bf16),
        ],
        "front",
        6 * bits * rank * rows * samples,
        8 * levels * rows * rank,
        room=FRONT,
        ins=[SMEM, HBM, HBM, HBM, HBM],
        scratch=[
            pltpu.VMEM((rows, samples), bf16),
            pltpu.VMEM((rows, leaf), bf16),
            pltpu.VMEM((levels, rows, rank), f32),
            pltpu.VMEM((max(1, len(inner)), rows, rank), f32),
            pltpu.VMEM((bits * rank, rows), bf16),
            pltpu.VMEM((bits * rank, rows), bf16),
            pltpu.SemaphoreType.DMA((2 + levels + max(1, len(inner)),)),
        ],
    )(core_s, residual_cols, leaf_inverse, basis_right, basis_left)
    got = swapped(send, 1)
    solved_other = swapped(solved_send, 1)
    left16 = call(
        functools.partial(left_kernel, bits, rank),
        out((rows, bits * rank), bf16),
        "left16",
        bits * rows * rank,
        6 * bits * rows * rank,
        room=24,
        ins=[HBM],
        scratch=[pltpu.VMEM((bits, rows, rank), f32), pltpu.SemaphoreType.DMA((bits,))],
    )(basis_left)
    left_other = swapped(left16, 1)

    shares, others = [None] * bits, [None] * bits
    top = bits - 1
    depth_of = lambda bit: max(16, 1 << (bit - 1))
    pairs_below = lambda level: level * (level - 1) // 2 * rank
    spot_rows = jnp.concatenate([map_pos, spot_other]).reshape(1, 2 * tile)
    y, message, last = call(
        functools.partial(first_merge, top, rank, depth_of(1)),
        [
            out((top * rank, half), f32),
            out((top * rank + 3 * depth_of(1), half), bf16),
            out((rank, half), bf16),
        ],
        "merge0",
        4 * top * rank * rank * half,
        8 * top * rank * half,
    )(keep, got, small, small_other, spot_rows)
    ahead = (1, 2)
    small_own, small_theirs = {}, {}
    previous = small, small_other
    for bit in ahead:
        kept = pairs_below(top - bit + 1)
        both = (previous[0][:kept].astype(f32) + previous[1][:kept].astype(f32)).astype(bf16)
        small_own[bit] = both
        small_theirs[bit] = swapped(both, 1 << bit)
        previous = small_own[bit], small_theirs[bit]
    shares[top] = got[top * rank :]
    others[top] = swapped(last, 1)
    points = [lax.dynamic_slice_in_dim(point_pos, s * rows, rows).reshape(blocks, leaf) for s in (me, me ^ 1)]
    points = jnp.concatenate(points, 0)
    info = jnp.concatenate(
        [me.reshape(1)]
        + [lax.dynamic_index_in_dim(t, s, 1, keepdims=False) for t in (block_first, block_count) for s in (me, me ^ 1)]
    )
    for bit in range(1, bits):
        level = top - bit
        arrived = swapped(message, 1 << bit)
        share = arrived[level * rank : (level + 1) * rank]
        shares[level] = share
        if level > 1:
            others[level] = swapped(share, 1)
        if level == 1:
            part_mine, part_other = call(
                functools.partial(partial_kernel, bits, rank),
                [out((rows, half), f32)] * 2,
                "partial",
                4 * bits * rows * rank * half,
                16 * rows * half,
            )(solved_mine, solved_other, left16, left_other, last, *shares[2:])
            arrived, part_mine, part_other, info, points, others[2:] = lax.optimization_barrier(
                (arrived, part_mine, part_other, info, points, others[2:])
            )
        if level:
            apart, along = bit in ahead, bit + 1 not in ahead
            inner_rows = pairs_below(level) if along else 0
            *kept_y, message = call(
                functools.partial(
                    merge, level, rank, apart, along, 1 << (bit - 1), (depth_of(bit), depth_of(bit + 1))
                ),
                [out((level * rank, half), f32)] * (level > 1)
                + [out((level * rank + inner_rows + 3 * depth_of(bit + 1), half), bf16)],
                f"merge{bit}",
                4 * level * rank * rank * half,
                8 * level * rank * half,
            )(y, message, arrived, *((small_own[bit], small_theirs[bit]) if apart else ()))
            y = kept_y[0] if kept_y else None

    plane = 4
    near = devices // (4 * plane)
    depth = depth_of(bits - 1)
    chips = 1 << (bits - 2)
    near_weights = call(
        functools.partial(near_kernel, plane, near, tile, leaf, blocks, devices, chips, depth, rank),
        [out((2 * near * tile, 2 * rows), bf16)] * plane,
        "near",
        40 * plane * near * tile * rows,
        8 * plane * near * tile * rows,
        room=8 if near <= 4 else 24,
        ins=[SMEM, VMEM, VMEM],
    )(info, message, points)
    final_mine, coeffs, spots = call(
        functools.partial(coeff_kernel, rank, chips, depth, 2.0 * leaf),
        [out((rows, half), f32), out((2 * rows, half), bf16), out((2 * tile, chips), f32)],
        "coeffs",
        4 * rows * rank * half,
        16 * rows * half,
    )(part_mine, part_other, left16, left_other, shares[1], arrived)

    def weighed(mask, coeffs):
        return call(
            functools.partial(far_kernel, mask, plane, near, tile, leaf, blocks, devices),
            out((4 * near * tile, half), bf16 if mask else f32),
            f"weigh{mask}",
            32 * near * tile * rows * half,
            32 * near * tile * half,
            room=8 if near <= 4 else 16,
            ins=[SMEM, VMEM, VMEM, VMEM, VMEM],
            scratch=[pltpu.VMEM((2 * near * tile, 2 * rows), bf16)],
        )(info, spots, near_weights[mask], points, coeffs)

    sent = []
    for mask in (3, 2, 1):
        if mask == 1:
            coeffs, others[:2] = lax.optimization_barrier((coeffs, others[:2]))
        partial = weighed(mask, coeffs)
        coeffs, partial = lax.optimization_barrier((coeffs, partial))
        if mask == 2:
            share0, share1, _ = lax.optimization_barrier((shares[0], shares[1], coeffs))
            others[:2] = swapped(share0, 1), swapped(share1, 1)
        sent.append(swapped(partial, mask << 1))
    solved_out = call(
        solved_kernel,
        out((rows, samples), f32),
        "solved",
        2 * bits * rows * rank * half,
        16 * rows * samples,
        ins=[SMEM] + [VMEM] * (3 + bits),
    )(core_s, final_mine, solved_send, left16, *others)
    coeffs, solved_out = lax.optimization_barrier((coeffs, solved_out))
    total = weighed(0, coeffs)
    for partial in sent:
        total = total + partial.astype(f32)
    far = 2 * near
    total = total.reshape(far, 2 * tile, half)
    result = total[0]
    for mask in range(1, far):
        result = result + swapped(total[mask].astype(bf16), mask << 3).astype(f32)
    rest = swapped(result[tile:], 1)

    mapped = jnp.where(
        core == 0,
        jnp.concatenate([result[:tile], rest], 1),
        jnp.concatenate([rest, result[:tile]], 1),
    )
    return (solved_out, prior_map.astype(f32) + mapped)


def solution(mesh):
    in_specs = (
        P(("groups", "pts"), None),
        P(("groups", "pts"), None),
        P(None, ("groups", "pts"), None),
        P(None, ("groups", "pts"), None),
        P(),
        P("pts"),
        P(("groups", "pts"), None),
        P(),
        P(),
    )
    out_specs = (P(("groups", "pts"), None), P(("groups", "pts"), None))
    return jax.shard_map(body, mesh=mesh, in_specs=in_specs, out_specs=out_specs, check_vma=False)
```

```python
import functools

import jax
import jax.numpy as jnp
from jax import lax
from jax.experimental import pallas as pl
from jax.experimental.pallas import tpu as pltpu
from jax.sharding import PartitionSpec as P

CAP = 2
amplitude = 0.2
bf16 = jnp.bfloat16
f32 = jnp.float32
MIB = 2**20
FRONT = 52.25
VMEM = pl.BlockSpec(memory_space=pltpu.VMEM)
SMEM = pl.BlockSpec(memory_space=pltpu.SMEM)
HBM = pl.BlockSpec(memory_space=pltpu.HBM)


def swapped(value, mask):
    pairs = [(source, source ^ mask) for source in range(lax.axis_size("pts"))]
    return lax.ppermute(value, "pts", pairs)


def call(kernel, outs, name, flops, moved, room=6, ins=None, scratch=()):
    more = {} if ins is None else {"in_specs": ins}
    return pl.pallas_call(
        kernel,
        out_shape=outs,
        name=name,
        compiler_params=pltpu.CompilerParams(vmem_limit_bytes=int(room * MIB)),
        scratch_shapes=list(scratch),
        cost_estimate=pl.CostEstimate(flops=flops, bytes_accessed=moved, transcendentals=0),
        **more,
    )


def dot(a, b):
    return jnp.dot(a, b, preferred_element_type=f32)


def two(value):
    high = value.astype(bf16)
    return high, (value - high.astype(f32)).astype(bf16)


def dot3(a, b):
    (ah, al), (bh, bl) = a, b
    return dot(ah, bh) + (dot(ah, bl) + dot(al, bh))


def out(shape, kind):
    return jax.ShapeDtypeStruct(shape, kind)


def small_kernel(bits, rank, right_ref, left_ref, small_ref, right_got, left_got, high_ref, sems):
    copies = []
    for i in range(bits - 1):
        copies.append(pltpu.make_async_copy(right_ref.at[i], right_got.at[i], sems.at[2 * i]))
        copies.append(pltpu.make_async_copy(left_ref.at[i + 1], left_got.at[i], sems.at[2 * i + 1]))
    for copy in copies:
        copy.start()
    for i in range(bits - 1):
        copies[2 * i].wait()
        high_ref[i * rank : (i + 1) * rank, :] = right_got[i].astype(bf16).T
        copies[2 * i + 1].wait()
        small_ref[small_at(i + 1, rank), :] = dot(
            high_ref[: (i + 1) * rank, :], left_got[i].astype(bf16)
        ).astype(bf16)


def left_kernel(bits, rank, left_ref, left16_ref, left_got, sems):
    copies = [pltpu.make_async_copy(left_ref.at[i], left_got.at[i], sems.at[i]) for i in range(bits)]
    for copy in copies:
        copy.start()
    for i in range(bits):
        copies[i].wait()
        left16_ref[:, i * rank : (i + 1) * rank] = left_got[i].astype(bf16)


def front_kernel(
    rows, leaf, bits, rank, levels, sizes, half, core_ref, residual_ref, inverse_ref, right_ref, left_ref,
    mine_ref, other_ref, keep_ref, message_ref,
    residual_got, inverse_got, right_got, left_got, high_ref, low_ref, sems,
):
    places = [(residual_ref, residual_got), (inverse_ref, inverse_got)]
    order = levels + list(range(bits))
    for level in order:
        places.append((right_ref.at[level], right_got.at[level]))
    for k, level in enumerate(levels):
        places.append((left_ref.at[level], left_got.at[k]))
    copies = [pltpu.make_async_copy(a, b, sems.at[k]) for k, (a, b) in enumerate(places)]
    for k in (0, 1, *range(2, 2 + len(levels)), *range(2 + len(order), len(places)), *range(2 + len(levels), 2 + len(order))):
        copies[k].start()
    right_copy = {level: copies[2 + k] for k, level in enumerate(order)}
    left_copy = copies[2 + len(order) :]
    copies[0].wait()
    copies[1].wait()
    x = [
        dot(inverse_got[b * leaf : (b + 1) * leaf, :], residual_got[b * leaf : (b + 1) * leaf, :])
        for b in range(rows // leaf)
    ]
    x = jnp.concatenate(x, 0)
    for k, (level, size) in enumerate(zip(levels, sizes)):
        right_copy[level].wait()
        projected = [
            dot3(two(right_got[level, a : a + size, :].T), two(x[a : a + size, :]))
            for a in range(0, rows, size)
        ]
        left_copy[k].wait()
        x = jnp.concatenate(
            [
                x[a * size : (a + 1) * size, :]
                + dot3(two(left_got[k, a * size : (a + 1) * size, :]), two(projected[a ^ 1]))
                for a in range(rows // size)
            ],
            0,
        )
    first = core_ref[0] == 0
    mine_ref[...] = jnp.where(first, x[:, :half], x[:, half:])
    other_ref[...] = jnp.where(first, x[:, half:], x[:, :half])
    xh, xl = two(x)
    for i in range(bits):
        right_copy[i].wait()
        at = slice(i * rank, (i + 1) * rank)
        high, low = two(right_got[i].T)
        high_ref[at, :] = high
        low_ref[at, :] = low
    a = dot(high_ref[...], xh) + (dot(high_ref[...], xl) + dot(low_ref[...], xh))
    keep_ref[...] = jnp.where(first, a[:, :half], a[:, half:])
    message_ref[...] = jnp.where(first, a[:, half:], a[:, :half]).astype(bf16)


def spread(value, depth):
    value = jnp.concatenate([value, jnp.zeros((depth - value.shape[0], value.shape[1]), f32)], 0) if depth > value.shape[0] else value
    one = value.astype(bf16)
    rest = value - one.astype(f32)
    second = rest.astype(bf16)
    return one, second, (rest - second.astype(f32)).astype(bf16)


def gathered(ref, at, depth):
    a = ref[at : at + depth, :].astype(f32)
    b = ref[at + depth : at + 2 * depth, :].astype(f32)
    return a + b + ref[at + 2 * depth : at + 3 * depth, :].astype(f32)


def put_spots(ref, at, depth, value):
    for k, part in enumerate(spread(value, depth)):
        ref[at + k * depth : at + (k + 1) * depth, :] = part


def linked(level, rank, own, theirs, own_small, their_small):
    cut = level * rank
    mine16, theirs16 = own[cut : cut + rank, :].astype(bf16), theirs[cut : cut + rank, :]
    return own[:cut, :] + theirs[:cut, :].astype(f32) + (dot(own_small, theirs16) + dot(their_small, mine16))


def small_at(level, rank):
    at = level * (level - 1) // 2 * rank
    return slice(at, at + level * rank)


def first_merge(level, rank, depth, keep_ref, got_ref, small_ref, their_ref, spot_ref, y_ref, message_ref):
    at = small_at(level, rank)
    y = linked(level, rank, keep_ref[...], got_ref[...], small_ref[at, :], their_ref[at, :])
    y_ref[...] = y
    cut = level * rank
    message_ref[:cut, :] = y.astype(bf16)
    put_spots(message_ref, cut, depth, spot_ref[...])


def merge(level, rank, apart, along, n, depths, y_in, own_ref, got_ref, *rest):
    own_small_ref, their_small_ref = rest[:2] if apart else (own_ref, got_ref)
    *y_ref, message_ref = rest[2:] if apart else rest
    base = 0 if apart else (level + 1) * rank
    spots_at = (level + 1) * rank + (0 if apart else level * (level + 1) // 2 * rank)
    at = small_at(level, rank)
    at = slice(base + at.start, base + at.stop)
    y = linked(level, rank, y_in[...], got_ref[...], own_small_ref[at, :], their_small_ref[at, :])
    if y_ref:
        y_ref[0][...] = y
    cut = level * rank
    message_ref[:cut, :] = y.astype(bf16)
    inner = level * (level - 1) // 2 * rank if along else 0
    if inner:
        total = own_small_ref[base : base + inner, :].astype(f32) + their_small_ref[base : base + inner, :].astype(f32)
        message_ref[cut : cut + inner, :] = total.astype(bf16)
    spots = jnp.concatenate(
        [gathered(own_ref, spots_at, depths[0])[:n, :], gathered(got_ref, spots_at, depths[0])[:n, :]], 0
    )
    put_spots(message_ref, cut + inner, depths[1], spots)


def partial_kernel(bits, rank, mine_ref, other_ref, left_ref, left_other_ref, last_ref, *refs):
    shares, outs = refs[: bits - 2], refs[bits - 2 :]
    top = [s[...] for s in shares[:-1]]
    outs[0][...] = mine_ref[...] + dot(left_ref[:, 2 * rank :], jnp.concatenate([s[...] for s in shares], 0))
    outs[1][...] = other_ref[...] + dot(left_other_ref[:, 2 * rank :], jnp.concatenate(top + [last_ref[...]], 0))


def coeff_kernel(rank, n, depth, scale, mine_ref, other_ref, left_ref, left_other_ref, share_ref, got_ref, final_ref, coeff_ref, spot_ref):
    rows = mine_ref.shape[0]
    share = jnp.concatenate([got_ref[:rank, :], share_ref[...]], 0)
    x = mine_ref[...] + dot(left_ref[:, : 2 * rank], share)
    final_ref[...] = x
    coeff_ref[:rows, :] = x.astype(bf16)
    coeff_ref[rows:, :] = (other_ref[...] + dot(left_other_ref[:, : 2 * rank], share)).astype(bf16)
    spot_ref[...] = (gathered(got_ref, rank, depth)[:n, :] * scale).T


def weigh(tile, leaf, blocks, devices, info_ref, spots, point_ref, weight_ref, q, column_at, at):
    scale = 2.0 * leaf
    for r in range(2):
        column = jnp.broadcast_to(spots[r * tile : (r + 1) * tile, column_at : column_at + 1], (tile, leaf))
        target = info_ref[0] ^ (2 * q + r)
        for s in range(2):
            first = info_ref[1 + s * devices + target]
            count = info_ref[1 + (2 + s) * devices + target]
            for k in range(CAP):
                block = s * blocks + first + k
                level = jnp.where(k < count, amplitude, 0.0)
                distance = jnp.minimum(jnp.abs(column - point_ref[pl.ds(block, 1), :] * scale), 1.0)
                left = 1.0 - distance
                left = left * left
                value = (left * left) * (1.0 + 4.0 * distance) * level
                lanes = pl.ds(pl.multiple_of(block * leaf, leaf), leaf)
                weight_ref[at + r * tile : at + (r + 1) * tile, lanes] = value.astype(bf16)


def near_kernel(plane, near, tile, leaf, blocks, devices, n, depth, rank, info_ref, own_ref, point_ref, *weight_refs):
    spots = (gathered(own_ref, rank, depth)[:n, :] * (2.0 * leaf)).T
    for mask in range(plane):
        weight_refs[mask][...] = jnp.zeros_like(weight_refs[mask])
        for z in range(near):
            q = mask + plane * z
            weigh(tile, leaf, blocks, devices, info_ref, spots, point_ref, weight_refs[mask], q, q, 2 * z * tile)


def far_kernel(mask, plane, near, tile, leaf, blocks, devices, info_ref, spot_ref, near_ref, point_ref, coeff_ref, out_ref, weight_ref):
    spots = spot_ref[...]
    weight_ref[...] = jnp.zeros_like(weight_ref)
    for z in range(near):
        column = mask + plane * z
        weigh(
            tile, leaf, blocks, devices, info_ref, spots, point_ref, weight_ref,
            column + plane * near, column, 2 * z * tile,
        )
    half = 2 * near * tile
    out_ref[:half, :] = dot(near_ref[...], coeff_ref[...]).astype(out_ref.dtype)
    out_ref[half:, :] = dot(weight_ref[...], coeff_ref[...]).astype(out_ref.dtype)


def solved_kernel(core_ref, mine_ref, rest_ref, left_ref, *refs):
    others, out_ref = refs[:-1], refs[-1]
    half = mine_ref.shape[1]
    x, y = mine_ref[...], rest_ref[...] + dot(left_ref[...], jnp.concatenate([s[...] for s in others], 0))
    first = core_ref[0] == 0
    out_ref[:, :half] = jnp.where(first, x, y)
    out_ref[:, half:] = jnp.where(first, y, x)


def body(
    residual_cols,
    leaf_inverse,
    basis_left,
    basis_right,
    point_pos,
    map_pos,
    prior_map,
    block_first,
    block_count,
):
    rows, samples = residual_cols.shape
    leaf = leaf_inverse.shape[1]
    rank = basis_left.shape[2]
    blocks = rows // leaf
    devices = lax.axis_size("pts")
    bits = devices.bit_length() - 1
    me = lax.axis_index("pts").astype(jnp.int32)
    core = me % 2
    core_s = core.reshape(1)
    levels = basis_left.shape[0]
    tile = map_pos.shape[0]
    half = samples // 2
    pair_count = bits * (bits - 1) // 2

    spot_other = swapped(map_pos, 1)
    inner = list(reversed(range(bits, levels)))
    sizes = [rows * devices // 2 ** (level + 1) for level in inner]
    small = call(
        functools.partial(small_kernel, bits, rank),
        out((pair_count * rank, rank), bf16),
        "small",
        2 * pair_count * rank * rank * rows,
        8 * bits * rows * rank,
        room=FRONT,
        ins=[HBM, HBM],
        scratch=[
            pltpu.VMEM((bits - 1, rows, rank), f32),
            pltpu.VMEM((bits - 1, rows, rank), f32),
            pltpu.VMEM(((bits - 1) * rank, rows), bf16),
            pltpu.SemaphoreType.DMA((2 * bits - 2,)),
        ],
    )(basis_right, basis_left)
    small_other = swapped(small, 1)
    solved_mine, solved_send, keep, send = call(
        functools.partial(front_kernel, rows, leaf, bits, rank, inner, sizes, half),
        [
            out((rows, half), f32),
            out((rows, half), f32),
            out((bits * rank, half), f32),
            out((bits * rank, half), bf16),
        ],
        "front",
        6 * bits * rank * rows * samples,
        8 * levels * rows * rank,
        room=FRONT,
        ins=[SMEM, HBM, HBM, HBM, HBM],
        scratch=[
            pltpu.VMEM((rows, samples), bf16),
            pltpu.VMEM((rows, leaf), bf16),
            pltpu.VMEM((levels, rows, rank), f32),
            pltpu.VMEM((max(1, len(inner)), rows, rank), f32),
            pltpu.VMEM((bits * rank, rows), bf16),
            pltpu.VMEM((bits * rank, rows), bf16),
            pltpu.SemaphoreType.DMA((2 + levels + max(1, len(inner)),)),
        ],
    )(core_s, residual_cols, leaf_inverse, basis_right, basis_left)
    got = swapped(send, 1)
    solved_other = swapped(solved_send, 1)
    left16 = call(
        functools.partial(left_kernel, bits, rank),
        out((rows, bits * rank), bf16),
        "left16",
        bits * rows * rank,
        6 * bits * rows * rank,
        room=24,
        ins=[HBM],
        scratch=[pltpu.VMEM((bits, rows, rank), f32), pltpu.SemaphoreType.DMA((bits,))],
    )(basis_left)
    left_other = swapped(left16, 1)

    shares, others = [None] * bits, [None] * bits
    top = bits - 1
    depth_of = lambda bit: max(16, 1 << (bit - 1))
    pairs_below = lambda level: level * (level - 1) // 2 * rank
    spot_rows = jnp.concatenate([map_pos, spot_other]).reshape(1, 2 * tile)
    y, message = call(
        functools.partial(first_merge, top, rank, depth_of(1)),
        [
            out((top * rank, half), f32),
            out((top * rank + 3 * depth_of(1), half), bf16),
        ],
        "merge0",
        4 * top * rank * rank * half,
        8 * top * rank * half,
    )(keep, got, small, small_other, spot_rows)
    ahead = (1, 2)
    small_own, small_theirs = {}, {}
    previous = small, small_other
    for bit in ahead:
        kept = pairs_below(top - bit + 1)
        both = (previous[0][:kept].astype(f32) + previous[1][:kept].astype(f32)).astype(bf16)
        small_own[bit] = both
        small_theirs[bit] = swapped(both, 1 << bit)
        previous = small_own[bit], small_theirs[bit]
    shares[top] = got[top * rank :]
    last = keep[top * rank :].astype(bf16)
    others[top] = swapped(last, 1)
    points = [lax.dynamic_slice_in_dim(point_pos, s * rows, rows).reshape(blocks, leaf) for s in (me, me ^ 1)]
    points = jnp.concatenate(points, 0)
    info = jnp.concatenate(
        [me.reshape(1)]
        + [lax.dynamic_index_in_dim(t, s, 1, keepdims=False) for t in (block_first, block_count) for s in (me, me ^ 1)]
    )
    for bit in range(1, bits):
        level = top - bit
        arrived = swapped(message, 1 << bit)
        share = arrived[level * rank : (level + 1) * rank]
        shares[level] = share
        if level > 1:
            others[level] = swapped(share, 1)
        if level == 1:
            part_mine, part_other = call(
                functools.partial(partial_kernel, bits, rank),
                [out((rows, half), f32)] * 2,
                "partial",
                4 * bits * rows * rank * half,
                16 * rows * half,
            )(solved_mine, solved_other, left16, left_other, last, *shares[2:])
            arrived, part_mine, part_other, info, points = lax.optimization_barrier(
                (arrived, part_mine, part_other, info, points)
            )
        if level:
            apart, along = bit in ahead, bit + 1 not in ahead
            inner_rows = pairs_below(level) if along else 0
            *kept_y, message = call(
                functools.partial(
                    merge, level, rank, apart, along, 1 << (bit - 1), (depth_of(bit), depth_of(bit + 1))
                ),
                [out((level * rank, half), f32)] * (level > 1)
                + [out((level * rank + inner_rows + 3 * depth_of(bit + 1), half), bf16)],
                f"merge{bit}",
                4 * level * rank * rank * half,
                8 * level * rank * half,
            )(y, message, arrived, *((small_own[bit], small_theirs[bit]) if apart else ()))
            y = kept_y[0] if kept_y else None

    plane = 4
    near = devices // (4 * plane)
    depth = depth_of(bits - 1)
    chips = 1 << (bits - 2)
    near_weights = call(
        functools.partial(near_kernel, plane, near, tile, leaf, blocks, devices, chips, depth, rank),
        [out((2 * near * tile, 2 * rows), bf16)] * plane,
        "near",
        40 * plane * near * tile * rows,
        8 * plane * near * tile * rows,
        room=8 if near <= 4 else 24,
        ins=[SMEM, VMEM, VMEM],
    )(info, message, points)
    final_mine, coeffs, spots = call(
        functools.partial(coeff_kernel, rank, chips, depth, 2.0 * leaf),
        [out((rows, half), f32), out((2 * rows, half), bf16), out((2 * tile, chips), f32)],
        "coeffs",
        4 * rows * rank * half,
        16 * rows * half,
    )(part_mine, part_other, left16, left_other, shares[1], arrived)

    def weighed(mask, coeffs):
        return call(
            functools.partial(far_kernel, mask, plane, near, tile, leaf, blocks, devices),
            out((4 * near * tile, half), bf16 if mask else f32),
            f"weigh{mask}",
            32 * near * tile * rows * half,
            32 * near * tile * half,
            room=8 if near <= 4 else 16,
            ins=[SMEM, VMEM, VMEM, VMEM, VMEM],
            scratch=[pltpu.VMEM((2 * near * tile, 2 * rows), bf16)],
        )(info, spots, near_weights[mask], points, coeffs)

    sent = []
    for mask in (3, 2, 1):
        if mask == 1:
            coeffs, others = lax.optimization_barrier((coeffs, others))
        partial = weighed(mask, coeffs)
        coeffs, partial = lax.optimization_barrier((coeffs, partial))
        if mask == 2:
            share0, share1, _ = lax.optimization_barrier((shares[0], shares[1], coeffs))
            others[:2] = swapped(share0, 1), swapped(share1, 1)
        sent.append(swapped(partial, mask << 1))
    solved_out = call(
        solved_kernel,
        out((rows, samples), f32),
        "solved",
        2 * bits * rows * rank * half,
        16 * rows * samples,
        ins=[SMEM] + [VMEM] * (3 + bits),
    )(core_s, final_mine, solved_send, left16, *others)
    coeffs, solved_out = lax.optimization_barrier((coeffs, solved_out))
    total = weighed(0, coeffs)
    for partial in sent:
        total = total + partial.astype(f32)
    far = 2 * near
    total = total.reshape(far, 2 * tile, half)
    result = total[0]
    for mask in range(1, far):
        result = result + swapped(total[mask].astype(bf16), mask << 3).astype(f32)
    rest = swapped(result[tile:], 1)

    mapped = jnp.where(
        core == 0,
        jnp.concatenate([result[:tile], rest], 1),
        jnp.concatenate([rest, result[:tile]], 1),
    )
    return (solved_out, prior_map.astype(f32) + mapped)


def solution(mesh):
    in_specs = (
        P(("groups", "pts"), None),
        P(("groups", "pts"), None),
        P(None, ("groups", "pts"), None),
        P(None, ("groups", "pts"), None),
        P(),
        P("pts"),
        P(("groups", "pts"), None),
        P(),
        P(),
    )
    out_specs = (P(("groups", "pts"), None), P(("groups", "pts"), None))
    return jax.shard_map(body, mesh=mesh, in_specs=in_specs, out_specs=out_specs, check_vma=False)
```

```python
import functools

import jax
import jax.numpy as jnp
from jax import lax
from jax.experimental import pallas as pl
from jax.experimental.pallas import tpu as pltpu
from jax.sharding import PartitionSpec as P

CAP = 2
amplitude = 0.2
bf16 = jnp.bfloat16
f32 = jnp.float32
MIB = 2**20
FRONT = 52.25
VMEM = pl.BlockSpec(memory_space=pltpu.VMEM)
SMEM = pl.BlockSpec(memory_space=pltpu.SMEM)
HBM = pl.BlockSpec(memory_space=pltpu.HBM)


def swapped(value, mask):
    pairs = [(source, source ^ mask) for source in range(lax.axis_size("pts"))]
    return lax.ppermute(value, "pts", pairs)


def call(kernel, outs, name, flops, moved, room=6, ins=None, scratch=()):
    more = {} if ins is None else {"in_specs": ins}
    return pl.pallas_call(
        kernel,
        out_shape=outs,
        name=name,
        compiler_params=pltpu.CompilerParams(vmem_limit_bytes=int(room * MIB)),
        scratch_shapes=list(scratch),
        cost_estimate=pl.CostEstimate(flops=flops, bytes_accessed=moved, transcendentals=0),
        **more,
    )


def dot(a, b):
    return jnp.dot(a, b, preferred_element_type=f32)


def two(value):
    high = value.astype(bf16)
    return high, (value - high.astype(f32)).astype(bf16)


def dot3(a, b):
    (ah, al), (bh, bl) = a, b
    return dot(ah, bh) + (dot(ah, bl) + dot(al, bh))


def out(shape, kind):
    return jax.ShapeDtypeStruct(shape, kind)


def small_kernel(bits, rank, right_ref, left_ref, small_ref, right_got, left_got, high_ref, sems):
    copies = []
    for i in range(bits - 1):
        copies.append(pltpu.make_async_copy(right_ref.at[i], right_got.at[i], sems.at[2 * i]))
        copies.append(pltpu.make_async_copy(left_ref.at[i + 1], left_got.at[i], sems.at[2 * i + 1]))
    for copy in copies:
        copy.start()
    for i in range(bits - 1):
        copies[2 * i].wait()
        high_ref[i * rank : (i + 1) * rank, :] = right_got[i].astype(bf16).T
        copies[2 * i + 1].wait()
        small_ref[small_at(i + 1, rank), :] = dot(
            high_ref[: (i + 1) * rank, :], left_got[i].astype(bf16)
        ).astype(bf16)


def left_kernel(bits, rank, left_ref, left16_ref, left_got, sems):
    copies = [pltpu.make_async_copy(left_ref.at[i], left_got.at[i], sems.at[i]) for i in range(bits)]
    for copy in copies:
        copy.start()
    for i in range(bits):
        copies[i].wait()
        left16_ref[:, i * rank : (i + 1) * rank] = left_got[i].astype(bf16)


def front_kernel(
    rows, leaf, bits, rank, levels, sizes, half, core_ref, residual_ref, inverse_ref, right_ref, left_ref,
    mine_ref, other_ref, keep_ref, message_ref,
    residual_got, inverse_got, right_got, left_got, high_ref, low_ref, sems,
):
    places = [(residual_ref, residual_got), (inverse_ref, inverse_got)]
    order = levels + list(range(bits))
    for level in order:
        places.append((right_ref.at[level], right_got.at[level]))
    for k, level in enumerate(levels):
        places.append((left_ref.at[level], left_got.at[k]))
    copies = [pltpu.make_async_copy(a, b, sems.at[k]) for k, (a, b) in enumerate(places)]
    for k in (0, 1, *range(2, 2 + len(levels)), *range(2 + len(order), len(places)), *range(2 + len(levels), 2 + len(order))):
        copies[k].start()
    right_copy = {level: copies[2 + k] for k, level in enumerate(order)}
    left_copy = copies[2 + len(order) :]
    copies[0].wait()
    copies[1].wait()
    x = [
        dot(inverse_got[b * leaf : (b + 1) * leaf, :], residual_got[b * leaf : (b + 1) * leaf, :])
        for b in range(rows // leaf)
    ]
    x = jnp.concatenate(x, 0)
    for k, (level, size) in enumerate(zip(levels, sizes)):
        right_copy[level].wait()
        projected = [
            dot3(two(right_got[level, a : a + size, :].T), two(x[a : a + size, :]))
            for a in range(0, rows, size)
        ]
        left_copy[k].wait()
        x = jnp.concatenate(
            [
                x[a * size : (a + 1) * size, :]
                + dot3(two(left_got[k, a * size : (a + 1) * size, :]), two(projected[a ^ 1]))
                for a in range(rows // size)
            ],
            0,
        )
    first = core_ref[0] == 0
    mine_ref[...] = jnp.where(first, x[:, :half], x[:, half:])
    other_ref[...] = jnp.where(first, x[:, half:], x[:, :half])
    xh, xl = two(x)
    for i in range(bits):
        right_copy[i].wait()
        at = slice(i * rank, (i + 1) * rank)
        high, low = two(right_got[i].T)
        high_ref[at, :] = high
        low_ref[at, :] = low
    a = dot(high_ref[...], xh) + (dot(high_ref[...], xl) + dot(low_ref[...], xh))
    keep_ref[...] = jnp.where(first, a[:, :half], a[:, half:])
    message_ref[...] = jnp.where(first, a[:, half:], a[:, :half]).astype(bf16)


def spread(value, depth):
    value = jnp.concatenate([value, jnp.zeros((depth - value.shape[0], value.shape[1]), f32)], 0) if depth > value.shape[0] else value
    one = value.astype(bf16)
    rest = value - one.astype(f32)
    second = rest.astype(bf16)
    return one, second, (rest - second.astype(f32)).astype(bf16)


def gathered(ref, at, depth):
    a = ref[at : at + depth, :].astype(f32)
    b = ref[at + depth : at + 2 * depth, :].astype(f32)
    return a + b + ref[at + 2 * depth : at + 3 * depth, :].astype(f32)


def put_spots(ref, at, depth, value):
    for k, part in enumerate(spread(value, depth)):
        ref[at + k * depth : at + (k + 1) * depth, :] = part


def linked(level, rank, own, theirs, own_small, their_small):
    cut = level * rank
    mine16, theirs16 = own[cut : cut + rank, :].astype(bf16), theirs[cut : cut + rank, :]
    return own[:cut, :] + theirs[:cut, :].astype(f32) + (dot(own_small, theirs16) + dot(their_small, mine16))


def small_at(level, rank):
    at = level * (level - 1) // 2 * rank
    return slice(at, at + level * rank)


def first_merge(level, rank, depth, keep_ref, got_ref, small_ref, their_ref, spot_ref, y_ref, message_ref):
    at = small_at(level, rank)
    y = linked(level, rank, keep_ref[...], got_ref[...], small_ref[at, :], their_ref[at, :])
    y_ref[...] = y
    cut = level * rank
    message_ref[:cut, :] = y.astype(bf16)
    put_spots(message_ref, cut, depth, spot_ref[...])


def merge(level, rank, apart, along, n, depths, y_in, own_ref, got_ref, *rest):
    own_small_ref, their_small_ref = rest[:2] if apart else (own_ref, got_ref)
    *y_ref, message_ref = rest[2:] if apart else rest
    base = 0 if apart else (level + 1) * rank
    spots_at = (level + 1) * rank + (0 if apart else level * (level + 1) // 2 * rank)
    at = small_at(level, rank)
    at = slice(base + at.start, base + at.stop)
    y = linked(level, rank, y_in[...], got_ref[...], own_small_ref[at, :], their_small_ref[at, :])
    if y_ref:
        y_ref[0][...] = y
    cut = level * rank
    message_ref[:cut, :] = y.astype(bf16)
    inner = level * (level - 1) // 2 * rank if along else 0
    if inner:
        total = own_small_ref[base : base + inner, :].astype(f32) + their_small_ref[base : base + inner, :].astype(f32)
        message_ref[cut : cut + inner, :] = total.astype(bf16)
    spots = jnp.concatenate(
        [gathered(own_ref, spots_at, depths[0])[:n, :], gathered(got_ref, spots_at, depths[0])[:n, :]], 0
    )
    put_spots(message_ref, cut + inner, depths[1], spots)


def partial_kernel(bits, rank, mine_ref, other_ref, left_ref, left_other_ref, last_ref, *refs):
    shares, outs = refs[: bits - 2], refs[bits - 2 :]
    top = [s[...] for s in shares[:-1]]
    outs[0][...] = mine_ref[...] + dot(left_ref[:, 2 * rank :], jnp.concatenate([s[...] for s in shares], 0))
    outs[1][...] = other_ref[...] + dot(left_other_ref[:, 2 * rank :], jnp.concatenate(top + [last_ref[...]], 0))


def coeff_kernel(rank, n, depth, scale, mine_ref, other_ref, left_ref, left_other_ref, share_ref, got_ref, final_ref, coeff_ref, spot_ref):
    rows = mine_ref.shape[0]
    share = jnp.concatenate([got_ref[:rank, :], share_ref[...]], 0)
    x = mine_ref[...] + dot(left_ref[:, : 2 * rank], share)
    final_ref[...] = x
    coeff_ref[:rows, :] = x.astype(bf16)
    coeff_ref[rows:, :] = (other_ref[...] + dot(left_other_ref[:, : 2 * rank], share)).astype(bf16)
    spot_ref[...] = (gathered(got_ref, rank, depth)[:n, :] * scale).T


def weigh(tile, leaf, blocks, devices, info_ref, spots, point_ref, weight_ref, q, column_at, at):
    scale = 2.0 * leaf
    for r in range(2):
        column = jnp.broadcast_to(spots[r * tile : (r + 1) * tile, column_at : column_at + 1], (tile, leaf))
        target = info_ref[0] ^ (2 * q + r)
        for s in range(2):
            first = info_ref[1 + s * devices + target]
            count = info_ref[1 + (2 + s) * devices + target]
            for k in range(CAP):
                block = s * blocks + first + k
                level = jnp.where(k < count, amplitude, 0.0)
                distance = jnp.minimum(jnp.abs(column - point_ref[pl.ds(block, 1), :] * scale), 1.0)
                left = 1.0 - distance
                left = left * left
                value = (left * left) * (1.0 + 4.0 * distance) * level
                lanes = pl.ds(pl.multiple_of(block * leaf, leaf), leaf)
                weight_ref[at + r * tile : at + (r + 1) * tile, lanes] = value.astype(bf16)


def near_kernel(plane, near, tile, leaf, blocks, devices, n, depth, rank, info_ref, own_ref, point_ref, *weight_refs):
    spots = (gathered(own_ref, rank, depth)[:n, :] * (2.0 * leaf)).T
    for mask in range(plane):
        weight_refs[mask][...] = jnp.zeros_like(weight_refs[mask])
        for z in range(near):
            q = mask + plane * z
            weigh(tile, leaf, blocks, devices, info_ref, spots, point_ref, weight_refs[mask], q, q, 2 * z * tile)


def far_kernel(mask, plane, near, tile, leaf, blocks, devices, info_ref, spot_ref, near_ref, point_ref, coeff_ref, out_ref, weight_ref):
    spots = spot_ref[...]
    weight_ref[...] = jnp.zeros_like(weight_ref)
    for z in range(near):
        column = mask + plane * z
        weigh(
            tile, leaf, blocks, devices, info_ref, spots, point_ref, weight_ref,
            column + plane * near, column, 2 * z * tile,
        )
    half = 2 * near * tile
    out_ref[:half, :] = dot(near_ref[...], coeff_ref[...]).astype(out_ref.dtype)
    out_ref[half:, :] = dot(weight_ref[...], coeff_ref[...]).astype(out_ref.dtype)


def first_kernel(rank, n, depth, scale, masks, shape, info_ref, point_ref, *refs):
    count = len(masks)
    inputs, near_refs, outs = refs[:6], refs[6 : 6 + count], refs[6 + count :]
    final_ref, coeff_ref, spot_ref = outs[:3]
    coeff_kernel(rank, n, depth, scale, *inputs, final_ref, coeff_ref, spot_ref)
    for k, mask in enumerate(masks):
        far_kernel(mask, *shape, info_ref, spot_ref, near_refs[k], point_ref, coeff_ref, outs[3 + k], outs[-1])


def solved_kernel(core_ref, mine_ref, rest_ref, left_ref, *refs):
    others, out_ref = refs[:-1], refs[-1]
    half = mine_ref.shape[1]
    x, y = mine_ref[...], rest_ref[...] + dot(left_ref[...], jnp.concatenate([s[...] for s in others], 0))
    first = core_ref[0] == 0
    out_ref[:, :half] = jnp.where(first, x, y)
    out_ref[:, half:] = jnp.where(first, y, x)


def body(
    residual_cols,
    leaf_inverse,
    basis_left,
    basis_right,
    point_pos,
    map_pos,
    prior_map,
    block_first,
    block_count,
):
    rows, samples = residual_cols.shape
    leaf = leaf_inverse.shape[1]
    rank = basis_left.shape[2]
    blocks = rows // leaf
    devices = lax.axis_size("pts")
    bits = devices.bit_length() - 1
    me = lax.axis_index("pts").astype(jnp.int32)
    core = me % 2
    core_s = core.reshape(1)
    levels = basis_left.shape[0]
    tile = map_pos.shape[0]
    half = samples // 2
    pair_count = bits * (bits - 1) // 2

    spot_other = swapped(map_pos, 1)
    inner = list(reversed(range(bits, levels)))
    sizes = [rows * devices // 2 ** (level + 1) for level in inner]
    small = call(
        functools.partial(small_kernel, bits, rank),
        out((pair_count * rank, rank), bf16),
        "small",
        2 * pair_count * rank * rank * rows,
        8 * bits * rows * rank,
        room=FRONT,
        ins=[HBM, HBM],
        scratch=[
            pltpu.VMEM((bits - 1, rows, rank), f32),
            pltpu.VMEM((bits - 1, rows, rank), f32),
            pltpu.VMEM(((bits - 1) * rank, rows), bf16),
            pltpu.SemaphoreType.DMA((2 * bits - 2,)),
        ],
    )(basis_right, basis_left)
    small_other = swapped(small, 1)
    solved_mine, solved_send, keep, send = call(
        functools.partial(front_kernel, rows, leaf, bits, rank, inner, sizes, half),
        [
            out((rows, half), f32),
            out((rows, half), f32),
            out((bits * rank, half), f32),
            out((bits * rank, half), bf16),
        ],
        "front",
        6 * bits * rank * rows * samples,
        8 * levels * rows * rank,
        room=FRONT,
        ins=[SMEM, HBM, HBM, HBM, HBM],
        scratch=[
            pltpu.VMEM((rows, samples), bf16),
            pltpu.VMEM((rows, leaf), bf16),
            pltpu.VMEM((levels, rows, rank), f32),
            pltpu.VMEM((max(1, len(inner)), rows, rank), f32),
            pltpu.VMEM((bits * rank, rows), bf16),
            pltpu.VMEM((bits * rank, rows), bf16),
            pltpu.SemaphoreType.DMA((2 + levels + max(1, len(inner)),)),
        ],
    )(core_s, residual_cols, leaf_inverse, basis_right, basis_left)
    got = swapped(send, 1)
    solved_other = swapped(solved_send, 1)
    left16 = call(
        functools.partial(left_kernel, bits, rank),
        out((rows, bits * rank), bf16),
        "left16",
        bits * rows * rank,
        6 * bits * rows * rank,
        room=24,
        ins=[HBM],
        scratch=[pltpu.VMEM((bits, rows, rank), f32), pltpu.SemaphoreType.DMA((bits,))],
    )(basis_left)
    left_other = swapped(left16, 1)

    shares, others = [None] * bits, [None] * bits
    top = bits - 1
    depth_of = lambda bit: max(16, 1 << (bit - 1))
    pairs_below = lambda level: level * (level - 1) // 2 * rank
    spot_rows = jnp.concatenate([map_pos, spot_other]).reshape(1, 2 * tile)
    y, message = call(
        functools.partial(first_merge, top, rank, depth_of(1)),
        [
            out((top * rank, half), f32),
            out((top * rank + 3 * depth_of(1), half), bf16),
        ],
        "merge0",
        4 * top * rank * rank * half,
        8 * top * rank * half,
    )(keep, got, small, small_other, spot_rows)
    ahead = (1, 2)
    small_own, small_theirs = {}, {}
    previous = small, small_other
    for bit in ahead:
        kept = pairs_below(top - bit + 1)
        both = (previous[0][:kept].astype(f32) + previous[1][:kept].astype(f32)).astype(bf16)
        small_own[bit] = both
        small_theirs[bit] = swapped(both, 1 << bit)
        previous = small_own[bit], small_theirs[bit]
    shares[top] = got[top * rank :]
    last = keep[top * rank :].astype(bf16)
    others[top] = swapped(last, 1)
    points = [lax.dynamic_slice_in_dim(point_pos, s * rows, rows).reshape(blocks, leaf) for s in (me, me ^ 1)]
    points = jnp.concatenate(points, 0)
    info = jnp.concatenate(
        [me.reshape(1)]
        + [lax.dynamic_index_in_dim(t, s, 1, keepdims=False) for t in (block_first, block_count) for s in (me, me ^ 1)]
    )
    for bit in range(1, bits):
        level = top - bit
        arrived = swapped(message, 1 << bit)
        share = arrived[level * rank : (level + 1) * rank]
        shares[level] = share
        if level > 1:
            others[level] = swapped(share, 1)
        if level == 1:
            part_mine, part_other = call(
                functools.partial(partial_kernel, bits, rank),
                [out((rows, half), f32)] * 2,
                "partial",
                4 * bits * rows * rank * half,
                16 * rows * half,
            )(solved_mine, solved_other, left16, left_other, last, *shares[2:])
            arrived, part_mine, part_other, info, points = lax.optimization_barrier(
                (arrived, part_mine, part_other, info, points)
            )
        if level:
            apart, along = bit in ahead, bit + 1 not in ahead
            inner_rows = pairs_below(level) if along else 0
            *kept_y, message = call(
                functools.partial(
                    merge, level, rank, apart, along, 1 << (bit - 1), (depth_of(bit), depth_of(bit + 1))
                ),
                [out((level * rank, half), f32)] * (level > 1)
                + [out((level * rank + inner_rows + 3 * depth_of(bit + 1), half), bf16)],
                f"merge{bit}",
                4 * level * rank * rank * half,
                8 * level * rank * half,
            )(y, message, arrived, *((small_own[bit], small_theirs[bit]) if apart else ()))
            y = kept_y[0] if kept_y else None

    plane = 4
    near = devices // (4 * plane)
    depth = depth_of(bits - 1)
    chips = 1 << (bits - 2)
    near_weights = call(
        functools.partial(near_kernel, plane, near, tile, leaf, blocks, devices, chips, depth, rank),
        [out((2 * near * tile, 2 * rows), bf16)] * plane,
        "near",
        40 * plane * near * tile * rows,
        8 * plane * near * tile * rows,
        room=8 if near <= 4 else 24,
        ins=[SMEM, VMEM, VMEM],
    )(info, message, points)
    early_masks = (3, 2)
    shape = plane, near, tile, leaf, blocks, devices
    final_mine, coeffs, spots, *partials = call(
        functools.partial(first_kernel, rank, chips, depth, 2.0 * leaf, early_masks, shape),
        [out((rows, half), f32), out((2 * rows, half), bf16), out((2 * tile, chips), f32)]
        + [out((4 * near * tile, half), bf16)] * len(early_masks),
        "first",
        64 * near * tile * rows * half,
        64 * near * tile * half,
        room=10 if near <= 4 else 24,
        ins=[SMEM] + [VMEM] * (7 + len(early_masks)),
        scratch=[pltpu.VMEM((2 * near * tile, 2 * rows), bf16)],
    )(
        info, points, part_mine, part_other, left16, left_other, shares[1], arrived,
        *[near_weights[mask] for mask in early_masks],
    )

    def weighed(mask, coeffs):
        return call(
            functools.partial(far_kernel, mask, *shape),
            out((4 * near * tile, half), bf16 if mask else f32),
            f"weigh{mask}",
            32 * near * tile * rows * half,
            32 * near * tile * half,
            room=8 if near <= 4 else 16,
            ins=[SMEM, VMEM, VMEM, VMEM, VMEM],
            scratch=[pltpu.VMEM((2 * near * tile, 2 * rows), bf16)],
        )(info, spots, near_weights[mask], points, coeffs)

    sent = [swapped(partial, mask << 1) for mask, partial in zip(early_masks, partials)]
    share0, share1, _ = lax.optimization_barrier((shares[0], shares[1], coeffs))
    others[:2] = swapped(share0, 1), swapped(share1, 1)
    coeffs, others = lax.optimization_barrier((coeffs, others))
    sent.append(swapped(weighed(1, coeffs), 1 << 1))
    solved_out = call(
        solved_kernel,
        out((rows, samples), f32),
        "solved",
        2 * bits * rows * rank * half,
        16 * rows * samples,
        ins=[SMEM] + [VMEM] * (3 + bits),
    )(core_s, final_mine, solved_send, left16, *others)
    coeffs, solved_out = lax.optimization_barrier((coeffs, solved_out))
    total = weighed(0, coeffs)
    for partial in sent:
        total = total + partial.astype(f32)
    far = 2 * near
    total = total.reshape(far, 2 * tile, half)
    result = total[0]
    for mask in reversed(range(1, far)):
        result = result + swapped(total[mask].astype(bf16), mask << 3).astype(f32)
    rest = swapped(result[tile:], 1)

    mapped = jnp.where(
        core == 0,
        jnp.concatenate([result[:tile], rest], 1),
        jnp.concatenate([rest, result[:tile]], 1),
    )
    return (solved_out, prior_map.astype(f32) + mapped)


def solution(mesh):
    in_specs = (
        P(("groups", "pts"), None),
        P(("groups", "pts"), None),
        P(None, ("groups", "pts"), None),
        P(None, ("groups", "pts"), None),
        P(),
        P("pts"),
        P(("groups", "pts"), None),
        P(),
        P(),
    )
    out_specs = (P(("groups", "pts"), None), P(("groups", "pts"), None))
    return jax.shard_map(body, mesh=mesh, in_specs=in_specs, out_specs=out_specs, check_vma=False)
```

```python
import functools

import jax
import jax.numpy as jnp
from jax import lax
from jax.experimental import pallas as pl
from jax.experimental.pallas import tpu as pltpu
from jax.sharding import PartitionSpec as P

CAP = 2
amplitude = 0.2
bf16 = jnp.bfloat16
f32 = jnp.float32
MIB = 2**20
FRONT = 52.25
VMEM = pl.BlockSpec(memory_space=pltpu.VMEM)
SMEM = pl.BlockSpec(memory_space=pltpu.SMEM)
HBM = pl.BlockSpec(memory_space=pltpu.HBM)


def swapped(value, mask):
    pairs = [(source, source ^ mask) for source in range(lax.axis_size("pts"))]
    return lax.ppermute(value, "pts", pairs)


def call(kernel, outs, name, flops, moved, room=6, ins=None, scratch=()):
    more = {} if ins is None else {"in_specs": ins}
    return pl.pallas_call(
        kernel,
        out_shape=outs,
        name=name,
        compiler_params=pltpu.CompilerParams(vmem_limit_bytes=int(room * MIB)),
        scratch_shapes=list(scratch),
        cost_estimate=pl.CostEstimate(flops=flops, bytes_accessed=moved, transcendentals=0),
        **more,
    )


def dot(a, b):
    return jnp.dot(a, b, preferred_element_type=f32)


def two(value):
    high = value.astype(bf16)
    return high, (value - high.astype(f32)).astype(bf16)


def dot3(a, b):
    (ah, al), (bh, bl) = a, b
    return dot(ah, bh) + (dot(ah, bl) + dot(al, bh))


def out(shape, kind):
    return jax.ShapeDtypeStruct(shape, kind)


def small_kernel(bits, rank, right_ref, left_ref, small_ref, right_got, left_got, high_ref, sems):
    copies = []
    for i in range(bits - 1):
        copies.append(pltpu.make_async_copy(right_ref.at[i], right_got.at[i], sems.at[2 * i]))
        copies.append(pltpu.make_async_copy(left_ref.at[i + 1], left_got.at[i], sems.at[2 * i + 1]))
    for copy in copies:
        copy.start()
    for i in range(bits - 1):
        copies[2 * i].wait()
        high_ref[i * rank : (i + 1) * rank, :] = right_got[i].astype(bf16).T
        copies[2 * i + 1].wait()
        small_ref[small_at(i + 1, rank), :] = dot(
            high_ref[: (i + 1) * rank, :], left_got[i].astype(bf16)
        ).astype(bf16)


def left_kernel(bits, rank, left_ref, left16_ref, left_got, sems):
    copies = [pltpu.make_async_copy(left_ref.at[i], left_got.at[i], sems.at[i]) for i in range(bits)]
    for copy in copies:
        copy.start()
    for i in range(bits):
        copies[i].wait()
        left16_ref[:, i * rank : (i + 1) * rank] = left_got[i].astype(bf16)


def front_kernel(
    rows, leaf, bits, rank, levels, sizes, half, core_ref, residual_ref, inverse_ref, right_ref, left_ref,
    mine_ref, other_ref, keep_ref, message_ref,
    residual_got, inverse_got, right_got, left_got, high_ref, low_ref, sems,
):
    places = [(residual_ref, residual_got), (inverse_ref, inverse_got)]
    order = levels + list(range(bits))
    for level in order:
        places.append((right_ref.at[level], right_got.at[level]))
    for k, level in enumerate(levels):
        places.append((left_ref.at[level], left_got.at[k]))
    copies = [pltpu.make_async_copy(a, b, sems.at[k]) for k, (a, b) in enumerate(places)]
    for k in (0, 1, *range(2, 2 + len(levels)), *range(2 + len(order), len(places)), *range(2 + len(levels), 2 + len(order))):
        copies[k].start()
    right_copy = {level: copies[2 + k] for k, level in enumerate(order)}
    left_copy = copies[2 + len(order) :]
    copies[0].wait()
    copies[1].wait()
    x = [
        dot(inverse_got[b * leaf : (b + 1) * leaf, :], residual_got[b * leaf : (b + 1) * leaf, :])
        for b in range(rows // leaf)
    ]
    x = jnp.concatenate(x, 0)
    for k, (level, size) in enumerate(zip(levels, sizes)):
        right_copy[level].wait()
        projected = [
            dot3(two(right_got[level, a : a + size, :].T), two(x[a : a + size, :]))
            for a in range(0, rows, size)
        ]
        left_copy[k].wait()
        x = jnp.concatenate(
            [
                x[a * size : (a + 1) * size, :]
                + dot3(two(left_got[k, a * size : (a + 1) * size, :]), two(projected[a ^ 1]))
                for a in range(rows // size)
            ],
            0,
        )
    first = core_ref[0] == 0
    mine_ref[...] = jnp.where(first, x[:, :half], x[:, half:])
    other_ref[...] = jnp.where(first, x[:, half:], x[:, :half])
    xh, xl = two(x)
    for i in range(bits):
        right_copy[i].wait()
        at = slice(i * rank, (i + 1) * rank)
        high, low = two(right_got[i].T)
        high_ref[at, :] = high
        low_ref[at, :] = low
    a = dot(high_ref[...], xh) + (dot(high_ref[...], xl) + dot(low_ref[...], xh))
    keep_ref[...] = jnp.where(first, a[:, :half], a[:, half:])
    message_ref[...] = jnp.where(first, a[:, half:], a[:, :half]).astype(bf16)


def spread(value, depth):
    value = jnp.concatenate([value, jnp.zeros((depth - value.shape[0], value.shape[1]), f32)], 0) if depth > value.shape[0] else value
    one = value.astype(bf16)
    rest = value - one.astype(f32)
    second = rest.astype(bf16)
    return one, second, (rest - second.astype(f32)).astype(bf16)


def gathered(ref, at, depth):
    a = ref[at : at + depth, :].astype(f32)
    b = ref[at + depth : at + 2 * depth, :].astype(f32)
    return a + b + ref[at + 2 * depth : at + 3 * depth, :].astype(f32)


def put_spots(ref, at, depth, value):
    for k, part in enumerate(spread(value, depth)):
        ref[at + k * depth : at + (k + 1) * depth, :] = part


def linked(level, rank, own, theirs, own_small, their_small):
    cut = level * rank
    mine16, theirs16 = own[cut : cut + rank, :].astype(bf16), theirs[cut : cut + rank, :]
    return own[:cut, :] + theirs[:cut, :].astype(f32) + (dot(own_small, theirs16) + dot(their_small, mine16))


def small_at(level, rank):
    at = level * (level - 1) // 2 * rank
    return slice(at, at + level * rank)


def first_merge(level, rank, depth, keep_ref, got_ref, small_ref, their_ref, spot_ref, y_ref, message_ref):
    at = small_at(level, rank)
    y = linked(level, rank, keep_ref[...], got_ref[...], small_ref[at, :], their_ref[at, :])
    y_ref[...] = y
    cut = level * rank
    message_ref[:cut, :] = y.astype(bf16)
    put_spots(message_ref, cut, depth, spot_ref[...])


def merge(level, rank, apart, along, n, depths, y_in, own_ref, got_ref, *rest):
    own_small_ref, their_small_ref = rest[:2] if apart else (own_ref, got_ref)
    *y_ref, message_ref = rest[2:] if apart else rest
    base = 0 if apart else (level + 1) * rank
    spots_at = (level + 1) * rank + (0 if apart else level * (level + 1) // 2 * rank)
    at = small_at(level, rank)
    at = slice(base + at.start, base + at.stop)
    y = linked(level, rank, y_in[...], got_ref[...], own_small_ref[at, :], their_small_ref[at, :])
    if y_ref:
        y_ref[0][...] = y
    cut = level * rank
    message_ref[:cut, :] = y.astype(bf16)
    inner = level * (level - 1) // 2 * rank if along else 0
    if inner:
        total = own_small_ref[base : base + inner, :].astype(f32) + their_small_ref[base : base + inner, :].astype(f32)
        message_ref[cut : cut + inner, :] = total.astype(bf16)
    spots = jnp.concatenate(
        [gathered(own_ref, spots_at, depths[0])[:n, :], gathered(got_ref, spots_at, depths[0])[:n, :]], 0
    )
    put_spots(message_ref, cut + inner, depths[1], spots)


def partial_kernel(bits, rank, mine_ref, other_ref, left_ref, left_other_ref, last_ref, *refs):
    shares, outs = refs[: bits - 2], refs[bits - 2 :]
    top = [s[...] for s in shares[:-1]]
    outs[0][...] = mine_ref[...] + dot(left_ref[:, 2 * rank :], jnp.concatenate([s[...] for s in shares], 0))
    outs[1][...] = other_ref[...] + dot(left_other_ref[:, 2 * rank :], jnp.concatenate(top + [last_ref[...]], 0))


def coeff_kernel(rank, n, depth, scale, mine_ref, other_ref, left_ref, left_other_ref, share_ref, got_ref, final_ref, coeff_ref, spot_ref):
    rows = mine_ref.shape[0]
    share = jnp.concatenate([got_ref[:rank, :], share_ref[...]], 0)
    x = mine_ref[...] + dot(left_ref[:, : 2 * rank], share)
    final_ref[...] = x
    coeff_ref[:rows, :] = x.astype(bf16)
    coeff_ref[rows:, :] = (other_ref[...] + dot(left_other_ref[:, : 2 * rank], share)).astype(bf16)
    spot_ref[...] = (gathered(got_ref, rank, depth)[:n, :] * scale).T


def weigh(tile, leaf, blocks, devices, info_ref, spots, point_ref, weight_ref, q, column_at, at):
    scale = 2.0 * leaf
    for r in range(2):
        column = jnp.broadcast_to(spots[r * tile : (r + 1) * tile, column_at : column_at + 1], (tile, leaf))
        target = info_ref[0] ^ (2 * q + r)
        for s in range(2):
            first = info_ref[1 + s * devices + target]
            count = info_ref[1 + (2 + s) * devices + target]
            for k in range(CAP):
                block = s * blocks + first + k
                level = jnp.where(k < count, amplitude, 0.0)
                distance = jnp.minimum(jnp.abs(column - point_ref[pl.ds(block, 1), :] * scale), 1.0)
                left = 1.0 - distance
                left = left * left
                value = (left * left) * (1.0 + 4.0 * distance) * level
                lanes = pl.ds(pl.multiple_of(block * leaf, leaf), leaf)
                weight_ref[at + r * tile : at + (r + 1) * tile, lanes] = value.astype(bf16)


def near_kernel(plane, near, tile, leaf, blocks, devices, n, depth, rank, info_ref, own_ref, point_ref, *weight_refs):
    spots = (gathered(own_ref, rank, depth)[:n, :] * (2.0 * leaf)).T
    for mask in range(plane):
        weight_refs[mask][...] = jnp.zeros_like(weight_refs[mask])
        for z in range(near):
            q = mask + plane * z
            weigh(tile, leaf, blocks, devices, info_ref, spots, point_ref, weight_refs[mask], q, q, 2 * z * tile)


def far_kernel(mask, plane, near, tile, leaf, blocks, devices, info_ref, spot_ref, near_ref, point_ref, coeff_ref, out_ref, weight_ref):
    spots = spot_ref[...]
    weight_ref[...] = jnp.zeros_like(weight_ref)
    for z in range(near):
        column = mask + plane * z
        weigh(
            tile, leaf, blocks, devices, info_ref, spots, point_ref, weight_ref,
            column + plane * near, column, 2 * z * tile,
        )
    half = 2 * near * tile
    out_ref[:half, :] = dot(near_ref[...], coeff_ref[...]).astype(out_ref.dtype)
    out_ref[half:, :] = dot(weight_ref[...], coeff_ref[...]).astype(out_ref.dtype)


def first_kernel(rank, n, depth, scale, masks, shape, info_ref, point_ref, *refs):
    count = len(masks)
    inputs, near_refs, outs = refs[:6], refs[6 : 6 + count], refs[6 + count :]
    final_ref, coeff_ref, spot_ref = outs[:3]
    coeff_kernel(rank, n, depth, scale, *inputs, final_ref, coeff_ref, spot_ref)
    for k, mask in enumerate(masks):
        far_kernel(mask, *shape, info_ref, spot_ref, near_refs[k], point_ref, coeff_ref, outs[3 + k], outs[-1])


def solved_kernel(core_ref, mine_ref, rest_ref, left_ref, *refs):
    others, out_ref = refs[:-1], refs[-1]
    half = mine_ref.shape[1]
    x, y = mine_ref[...], rest_ref[...] + dot(left_ref[...], jnp.concatenate([s[...] for s in others], 0))
    first = core_ref[0] == 0
    out_ref[:, :half] = jnp.where(first, x, y)
    out_ref[:, half:] = jnp.where(first, y, x)


def body(
    residual_cols,
    leaf_inverse,
    basis_left,
    basis_right,
    point_pos,
    map_pos,
    prior_map,
    block_first,
    block_count,
):
    rows, samples = residual_cols.shape
    leaf = leaf_inverse.shape[1]
    rank = basis_left.shape[2]
    blocks = rows // leaf
    devices = lax.axis_size("pts")
    bits = devices.bit_length() - 1
    me = lax.axis_index("pts").astype(jnp.int32)
    core = me % 2
    core_s = core.reshape(1)
    levels = basis_left.shape[0]
    tile = map_pos.shape[0]
    half = samples // 2
    pair_count = bits * (bits - 1) // 2

    spot_other = swapped(map_pos, 1)
    inner = list(reversed(range(bits, levels)))
    sizes = [rows * devices // 2 ** (level + 1) for level in inner]
    small = call(
        functools.partial(small_kernel, bits, rank),
        out((pair_count * rank, rank), bf16),
        "small",
        2 * pair_count * rank * rank * rows,
        8 * bits * rows * rank,
        room=FRONT,
        ins=[HBM, HBM],
        scratch=[
            pltpu.VMEM((bits - 1, rows, rank), f32),
            pltpu.VMEM((bits - 1, rows, rank), f32),
            pltpu.VMEM(((bits - 1) * rank, rows), bf16),
            pltpu.SemaphoreType.DMA((2 * bits - 2,)),
        ],
    )(basis_right, basis_left)
    small_other = swapped(small, 1)
    solved_mine, solved_send, keep, send = call(
        functools.partial(front_kernel, rows, leaf, bits, rank, inner, sizes, half),
        [
            out((rows, half), f32),
            out((rows, half), f32),
            out((bits * rank, half), f32),
            out((bits * rank, half), bf16),
        ],
        "front",
        6 * bits * rank * rows * samples,
        8 * levels * rows * rank,
        room=FRONT,
        ins=[SMEM, HBM, HBM, HBM, HBM],
        scratch=[
            pltpu.VMEM((rows, samples), bf16),
            pltpu.VMEM((rows, leaf), bf16),
            pltpu.VMEM((levels, rows, rank), f32),
            pltpu.VMEM((max(1, len(inner)), rows, rank), f32),
            pltpu.VMEM((bits * rank, rows), bf16),
            pltpu.VMEM((bits * rank, rows), bf16),
            pltpu.SemaphoreType.DMA((2 + levels + max(1, len(inner)),)),
        ],
    )(core_s, residual_cols, leaf_inverse, basis_right, basis_left)
    got = swapped(send, 1)
    solved_other = swapped(solved_send, 1)
    left16 = call(
        functools.partial(left_kernel, bits, rank),
        out((rows, bits * rank), bf16),
        "left16",
        bits * rows * rank,
        6 * bits * rows * rank,
        room=24,
        ins=[HBM],
        scratch=[pltpu.VMEM((bits, rows, rank), f32), pltpu.SemaphoreType.DMA((bits,))],
    )(basis_left)
    left_other = swapped(left16, 1)

    shares, others = [None] * bits, [None] * bits
    top = bits - 1
    depth_of = lambda bit: max(16, 1 << (bit - 1))
    pairs_below = lambda level: level * (level - 1) // 2 * rank
    spot_rows = jnp.concatenate([map_pos, spot_other]).reshape(1, 2 * tile)
    y, message = call(
        functools.partial(first_merge, top, rank, depth_of(1)),
        [
            out((top * rank, half), f32),
            out((top * rank + 3 * depth_of(1), half), bf16),
        ],
        "merge0",
        4 * top * rank * rank * half,
        8 * top * rank * half,
    )(keep, got, small, small_other, spot_rows)
    ahead = (1, 2)
    small_own, small_theirs = {}, {}
    previous = small, small_other
    for bit in ahead:
        kept = pairs_below(top - bit + 1)
        both = (previous[0][:kept].astype(f32) + previous[1][:kept].astype(f32)).astype(bf16)
        small_own[bit] = both
        small_theirs[bit] = swapped(both, 1 << bit)
        previous = small_own[bit], small_theirs[bit]
    shares[top] = got[top * rank :]
    last = keep[top * rank :].astype(bf16)
    others[top] = swapped(last, 1)
    points = [lax.dynamic_slice_in_dim(point_pos, s * rows, rows).reshape(blocks, leaf) for s in (me, me ^ 1)]
    points = jnp.concatenate(points, 0)
    info = jnp.concatenate(
        [me.reshape(1)]
        + [lax.dynamic_index_in_dim(t, s, 1, keepdims=False) for t in (block_first, block_count) for s in (me, me ^ 1)]
    )
    for bit in range(1, bits):
        level = top - bit
        arrived = swapped(message, 1 << bit)
        share = arrived[level * rank : (level + 1) * rank]
        shares[level] = share
        if level > 1:
            others[level] = swapped(share, 1)
        if level == 1:
            part_mine, part_other = call(
                functools.partial(partial_kernel, bits, rank),
                [out((rows, half), f32)] * 2,
                "partial",
                4 * bits * rows * rank * half,
                16 * rows * half,
            )(solved_mine, solved_other, left16, left_other, last, *shares[2:])
            arrived, part_mine, part_other, info, points = lax.optimization_barrier(
                (arrived, part_mine, part_other, info, points)
            )
        if level:
            apart, along = bit in ahead, bit + 1 not in ahead
            inner_rows = pairs_below(level) if along else 0
            *kept_y, message = call(
                functools.partial(
                    merge, level, rank, apart, along, 1 << (bit - 1), (depth_of(bit), depth_of(bit + 1))
                ),
                [out((level * rank, half), f32)] * (level > 1)
                + [out((level * rank + inner_rows + 3 * depth_of(bit + 1), half), bf16)],
                f"merge{bit}",
                4 * level * rank * rank * half,
                8 * level * rank * half,
            )(y, message, arrived, *((small_own[bit], small_theirs[bit]) if apart else ()))
            y = kept_y[0] if kept_y else None

    plane = 4
    near = devices // (4 * plane)
    depth = depth_of(bits - 1)
    chips = 1 << (bits - 2)
    near_weights = call(
        functools.partial(near_kernel, plane, near, tile, leaf, blocks, devices, chips, depth, rank),
        [out((2 * near * tile, 2 * rows), bf16)] * plane,
        "near",
        40 * plane * near * tile * rows,
        8 * plane * near * tile * rows,
        room=8 if near <= 4 else 24,
        ins=[SMEM, VMEM, VMEM],
    )(info, message, points)
    early_masks = (3, 2, 1)
    shape = plane, near, tile, leaf, blocks, devices
    final_mine, coeffs, spots, *partials = call(
        functools.partial(first_kernel, rank, chips, depth, 2.0 * leaf, early_masks, shape),
        [out((rows, half), f32), out((2 * rows, half), bf16), out((2 * tile, chips), f32)]
        + [out((4 * near * tile, half), bf16)] * len(early_masks),
        "first",
        64 * near * tile * rows * half,
        64 * near * tile * half,
        room=12 if near <= 4 else 28,
        ins=[SMEM] + [VMEM] * (7 + len(early_masks)),
        scratch=[pltpu.VMEM((2 * near * tile, 2 * rows), bf16)],
    )(
        info, points, part_mine, part_other, left16, left_other, shares[1], arrived,
        *[near_weights[mask] for mask in early_masks],
    )

    def weighed(mask, coeffs):
        return call(
            functools.partial(far_kernel, mask, *shape),
            out((4 * near * tile, half), bf16 if mask else f32),
            f"weigh{mask}",
            32 * near * tile * rows * half,
            32 * near * tile * half,
            room=8 if near <= 4 else 16,
            ins=[SMEM, VMEM, VMEM, VMEM, VMEM],
            scratch=[pltpu.VMEM((2 * near * tile, 2 * rows), bf16)],
        )(info, spots, near_weights[mask], points, coeffs)

    sent = [swapped(partial, mask << 1) for mask, partial in zip(early_masks, partials)]
    share0, share1, _ = lax.optimization_barrier((shares[0], shares[1], coeffs))
    others[:2] = swapped(share0, 1), swapped(share1, 1)
    solved_out = call(
        solved_kernel,
        out((rows, samples), f32),
        "solved",
        2 * bits * rows * rank * half,
        16 * rows * samples,
        ins=[SMEM] + [VMEM] * (3 + bits),
    )(core_s, final_mine, solved_send, left16, *others)
    coeffs, solved_out = lax.optimization_barrier((coeffs, solved_out))
    total = weighed(0, coeffs)
    for partial in sent:
        total = total + partial.astype(f32)
    far = 2 * near
    total = total.reshape(far, 2 * tile, half)
    result = total[0]
    for mask in reversed(range(1, far)):
        result = result + swapped(total[mask].astype(bf16), mask << 3).astype(f32)
    rest = swapped(result[tile:], 1)

    mapped = jnp.where(
        core == 0,
        jnp.concatenate([result[:tile], rest], 1),
        jnp.concatenate([rest, result[:tile]], 1),
    )
    return (solved_out, prior_map.astype(f32) + mapped)


def solution(mesh):
    in_specs = (
        P(("groups", "pts"), None),
        P(("groups", "pts"), None),
        P(None, ("groups", "pts"), None),
        P(None, ("groups", "pts"), None),
        P(),
        P("pts"),
        P(("groups", "pts"), None),
        P(),
        P(),
    )
    out_specs = (P(("groups", "pts"), None), P(("groups", "pts"), None))
    return jax.shard_map(body, mesh=mesh, in_specs=in_specs, out_specs=out_specs, check_vma=False)
```

```python
import functools

import jax
import jax.numpy as jnp
from jax import lax
from jax.experimental import pallas as pl
from jax.experimental.pallas import tpu as pltpu
from jax.sharding import PartitionSpec as P

CAP = 2
amplitude = 0.2
bf16 = jnp.bfloat16
f32 = jnp.float32
MIB = 2**20
FRONT = 52.25
VMEM = pl.BlockSpec(memory_space=pltpu.VMEM)
SMEM = pl.BlockSpec(memory_space=pltpu.SMEM)
HBM = pl.BlockSpec(memory_space=pltpu.HBM)


def swapped(value, mask):
    pairs = [(source, source ^ mask) for source in range(lax.axis_size("pts"))]
    return lax.ppermute(value, "pts", pairs)


def call(kernel, outs, name, flops, moved, room=6, ins=None, scratch=()):
    more = {} if ins is None else {"in_specs": ins}
    return pl.pallas_call(
        kernel,
        out_shape=outs,
        name=name,
        compiler_params=pltpu.CompilerParams(vmem_limit_bytes=int(room * MIB)),
        scratch_shapes=list(scratch),
        cost_estimate=pl.CostEstimate(flops=flops, bytes_accessed=moved, transcendentals=0),
        **more,
    )


def dot(a, b):
    return jnp.dot(a, b, preferred_element_type=f32)


def two(value):
    high = value.astype(bf16)
    return high, (value - high.astype(f32)).astype(bf16)


def dot3(a, b):
    (ah, al), (bh, bl) = a, b
    return dot(ah, bh) + (dot(ah, bl) + dot(al, bh))


def out(shape, kind):
    return jax.ShapeDtypeStruct(shape, kind)


def small_kernel(bits, rank, right_ref, left_ref, small_ref, right_got, left_got, high_ref, sems):
    copies = []
    for i in range(bits - 1):
        copies.append(pltpu.make_async_copy(right_ref.at[i], right_got.at[i], sems.at[2 * i]))
        copies.append(pltpu.make_async_copy(left_ref.at[i + 1], left_got.at[i], sems.at[2 * i + 1]))
    for copy in copies:
        copy.start()
    for i in range(bits - 1):
        copies[2 * i].wait()
        high_ref[i * rank : (i + 1) * rank, :] = right_got[i].astype(bf16).T
        copies[2 * i + 1].wait()
        small_ref[small_at(i + 1, rank), :] = dot(
            high_ref[: (i + 1) * rank, :], left_got[i].astype(bf16)
        ).astype(bf16)


def left_kernel(bits, rank, left_ref, left16_ref, left_got, sems):
    copies = [pltpu.make_async_copy(left_ref.at[i], left_got.at[i], sems.at[i]) for i in range(bits)]
    for copy in copies:
        copy.start()
    for i in range(bits):
        copies[i].wait()
        left16_ref[:, i * rank : (i + 1) * rank] = left_got[i].astype(bf16)


def front_kernel(
    rows, leaf, bits, rank, levels, sizes, half, core_ref, residual_ref, inverse_ref, right_ref, left_ref,
    mine_ref, other_ref, keep_ref, message_ref,
    residual_got, inverse_got, right_got, left_got, high_ref, low_ref, sems,
):
    places = [(residual_ref, residual_got), (inverse_ref, inverse_got)]
    order = levels + list(range(bits))
    for level in order:
        places.append((right_ref.at[level], right_got.at[level]))
    for k, level in enumerate(levels):
        places.append((left_ref.at[level], left_got.at[k]))
    copies = [pltpu.make_async_copy(a, b, sems.at[k]) for k, (a, b) in enumerate(places)]
    for k in (0, 1, *range(2, 2 + len(levels)), *range(2 + len(order), len(places)), *range(2 + len(levels), 2 + len(order))):
        copies[k].start()
    right_copy = {level: copies[2 + k] for k, level in enumerate(order)}
    left_copy = copies[2 + len(order) :]
    copies[0].wait()
    copies[1].wait()
    x = [
        dot(inverse_got[b * leaf : (b + 1) * leaf, :], residual_got[b * leaf : (b + 1) * leaf, :])
        for b in range(rows // leaf)
    ]
    x = jnp.concatenate(x, 0)
    for k, (level, size) in enumerate(zip(levels, sizes)):
        right_copy[level].wait()
        projected = [
            dot3(two(right_got[level, a : a + size, :].T), two(x[a : a + size, :]))
            for a in range(0, rows, size)
        ]
        left_copy[k].wait()
        x = jnp.concatenate(
            [
                x[a * size : (a + 1) * size, :]
                + dot3(two(left_got[k, a * size : (a + 1) * size, :]), two(projected[a ^ 1]))
                for a in range(rows // size)
            ],
            0,
        )
    first = core_ref[0] == 0
    mine_ref[...] = jnp.where(first, x[:, :half], x[:, half:])
    other_ref[...] = jnp.where(first, x[:, half:], x[:, :half])
    xh, xl = two(x)
    for i in range(bits):
        right_copy[i].wait()
        at = slice(i * rank, (i + 1) * rank)
        high, low = two(right_got[i].T)
        high_ref[at, :] = high
        low_ref[at, :] = low
    a = dot(high_ref[...], xh) + (dot(high_ref[...], xl) + dot(low_ref[...], xh))
    keep_ref[...] = jnp.where(first, a[:, :half], a[:, half:])
    message_ref[...] = jnp.where(first, a[:, half:], a[:, :half]).astype(bf16)


def spread(value, depth):
    value = jnp.concatenate([value, jnp.zeros((depth - value.shape[0], value.shape[1]), f32)], 0) if depth > value.shape[0] else value
    one = value.astype(bf16)
    rest = value - one.astype(f32)
    second = rest.astype(bf16)
    return one, second, (rest - second.astype(f32)).astype(bf16)


def gathered(ref, at, depth):
    a = ref[at : at + depth, :].astype(f32)
    b = ref[at + depth : at + 2 * depth, :].astype(f32)
    return a + b + ref[at + 2 * depth : at + 3 * depth, :].astype(f32)


def put_spots(ref, at, depth, value):
    for k, part in enumerate(spread(value, depth)):
        ref[at + k * depth : at + (k + 1) * depth, :] = part


def linked(level, rank, own, theirs, own_small, their_small):
    cut = level * rank
    mine16, theirs16 = own[cut : cut + rank, :].astype(bf16), theirs[cut : cut + rank, :]
    return own[:cut, :] + theirs[:cut, :].astype(f32) + (dot(own_small, theirs16) + dot(their_small, mine16))


def small_at(level, rank):
    at = level * (level - 1) // 2 * rank
    return slice(at, at + level * rank)


def first_merge(level, rank, depth, keep_ref, got_ref, small_ref, their_ref, spot_ref, y_ref, message_ref):
    at = small_at(level, rank)
    y = linked(level, rank, keep_ref[...], got_ref[...], small_ref[at, :], their_ref[at, :])
    y_ref[...] = y
    cut = level * rank
    message_ref[:cut, :] = y.astype(bf16)
    put_spots(message_ref, cut, depth, spot_ref[...])


def merge(level, rank, apart, along, n, depths, y_in, own_ref, got_ref, *rest):
    own_small_ref, their_small_ref = rest[:2] if apart else (own_ref, got_ref)
    *y_ref, message_ref = rest[2:] if apart else rest
    base = 0 if apart else (level + 1) * rank
    spots_at = (level + 1) * rank + (0 if apart else level * (level + 1) // 2 * rank)
    at = small_at(level, rank)
    at = slice(base + at.start, base + at.stop)
    y = linked(level, rank, y_in[...], got_ref[...], own_small_ref[at, :], their_small_ref[at, :])
    if y_ref:
        y_ref[0][...] = y
    cut = level * rank
    message_ref[:cut, :] = y.astype(bf16)
    inner = level * (level - 1) // 2 * rank if along else 0
    if inner:
        total = own_small_ref[base : base + inner, :].astype(f32) + their_small_ref[base : base + inner, :].astype(f32)
        message_ref[cut : cut + inner, :] = total.astype(bf16)
    spots = jnp.concatenate(
        [gathered(own_ref, spots_at, depths[0])[:n, :], gathered(got_ref, spots_at, depths[0])[:n, :]], 0
    )
    put_spots(message_ref, cut + inner, depths[1], spots)


def partial_kernel(bits, rank, mine_ref, other_ref, left_ref, left_other_ref, last_ref, *refs):
    shares, outs = refs[: bits - 2], refs[bits - 2 :]
    top = [s[...] for s in shares[:-1]]
    outs[0][...] = mine_ref[...] + dot(left_ref[:, 2 * rank :], jnp.concatenate([s[...] for s in shares], 0))
    outs[1][...] = other_ref[...] + dot(left_other_ref[:, 2 * rank :], jnp.concatenate(top + [last_ref[...]], 0))


def coeff_kernel(rank, n, depth, scale, mine_ref, other_ref, left_ref, left_other_ref, share_ref, got_ref, final_ref, coeff_ref, spot_ref):
    rows = mine_ref.shape[0]
    share = jnp.concatenate([got_ref[:rank, :], share_ref[...]], 0)
    x = mine_ref[...] + dot(left_ref[:, : 2 * rank], share)
    final_ref[...] = x
    coeff_ref[:rows, :] = x.astype(bf16)
    coeff_ref[rows:, :] = (other_ref[...] + dot(left_other_ref[:, : 2 * rank], share)).astype(bf16)
    spot_ref[...] = (gathered(got_ref, rank, depth)[:n, :] * scale).T


def weigh(tile, leaf, blocks, devices, info_ref, spots, point_ref, weight_ref, q, column_at, at):
    scale = 2.0 * leaf
    for r in range(2):
        column = jnp.broadcast_to(spots[r * tile : (r + 1) * tile, column_at : column_at + 1], (tile, leaf))
        target = info_ref[0] ^ (2 * q + r)
        for s in range(2):
            first = info_ref[1 + s * devices + target]
            count = info_ref[1 + (2 + s) * devices + target]
            for k in range(CAP):
                block = s * blocks + first + k
                level = jnp.where(k < count, amplitude, 0.0)
                distance = jnp.minimum(jnp.abs(column - point_ref[pl.ds(block, 1), :] * scale), 1.0)
                left = 1.0 - distance
                left = left * left
                value = (left * left) * (1.0 + 4.0 * distance) * level
                lanes = pl.ds(pl.multiple_of(block * leaf, leaf), leaf)
                weight_ref[at + r * tile : at + (r + 1) * tile, lanes] = value.astype(bf16)


def near_kernel(plane, near, tile, leaf, blocks, devices, n, depth, rank, info_ref, own_ref, point_ref, *weight_refs):
    spots = (gathered(own_ref, rank, depth)[:n, :] * (2.0 * leaf)).T
    for mask in range(plane):
        weight_refs[mask][...] = jnp.zeros_like(weight_refs[mask])
        for z in range(near):
            q = mask + plane * z
            weigh(tile, leaf, blocks, devices, info_ref, spots, point_ref, weight_refs[mask], q, q, 2 * z * tile)


def far_kernel(mask, plane, near, tile, leaf, blocks, devices, info_ref, spot_ref, near_ref, point_ref, coeff_ref, out_ref, weight_ref):
    spots = spot_ref[...]
    weight_ref[...] = jnp.zeros_like(weight_ref)
    for z in range(near):
        column = mask + plane * z
        weigh(
            tile, leaf, blocks, devices, info_ref, spots, point_ref, weight_ref,
            column + plane * near, column, 2 * z * tile,
        )
    half = 2 * near * tile
    out_ref[:half, :] = dot(near_ref[...], coeff_ref[...]).astype(out_ref.dtype)
    out_ref[half:, :] = dot(weight_ref[...], coeff_ref[...]).astype(out_ref.dtype)


def first_kernel(rank, n, depth, scale, masks, shape, info_ref, point_ref, *refs):
    count = len(masks)
    inputs, near_refs, outs = refs[:6], refs[6 : 6 + count], refs[6 + count :]
    final_ref, coeff_ref, spot_ref = outs[:3]
    coeff_kernel(rank, n, depth, scale, *inputs, final_ref, coeff_ref, spot_ref)
    for k, mask in enumerate(masks):
        far_kernel(mask, *shape, info_ref, spot_ref, near_refs[k], point_ref, coeff_ref, outs[3 + k], outs[-1])


def solved_kernel(core_ref, mine_ref, rest_ref, left_ref, *refs):
    others, out_ref = refs[:-1], refs[-1]
    half = mine_ref.shape[1]
    x, y = mine_ref[...], rest_ref[...] + dot(left_ref[...], jnp.concatenate([s[...] for s in others], 0))
    first = core_ref[0] == 0
    out_ref[:, :half] = jnp.where(first, x, y)
    out_ref[:, half:] = jnp.where(first, y, x)


def body(
    residual_cols,
    leaf_inverse,
    basis_left,
    basis_right,
    point_pos,
    map_pos,
    prior_map,
    block_first,
    block_count,
):
    rows, samples = residual_cols.shape
    leaf = leaf_inverse.shape[1]
    rank = basis_left.shape[2]
    blocks = rows // leaf
    devices = lax.axis_size("pts")
    bits = devices.bit_length() - 1
    me = lax.axis_index("pts").astype(jnp.int32)
    core = me % 2
    core_s = core.reshape(1)
    levels = basis_left.shape[0]
    tile = map_pos.shape[0]
    half = samples // 2
    pair_count = bits * (bits - 1) // 2

    spot_other = swapped(map_pos, 1)
    inner = list(reversed(range(bits, levels)))
    sizes = [rows * devices // 2 ** (level + 1) for level in inner]
    small = call(
        functools.partial(small_kernel, bits, rank),
        out((pair_count * rank, rank), bf16),
        "small",
        2 * pair_count * rank * rank * rows,
        8 * bits * rows * rank,
        room=FRONT,
        ins=[HBM, HBM],
        scratch=[
            pltpu.VMEM((bits - 1, rows, rank), f32),
            pltpu.VMEM((bits - 1, rows, rank), f32),
            pltpu.VMEM(((bits - 1) * rank, rows), bf16),
            pltpu.SemaphoreType.DMA((2 * bits - 2,)),
        ],
    )(basis_right, basis_left)
    small_other = swapped(small, 1)
    solved_mine, solved_send, keep, send = call(
        functools.partial(front_kernel, rows, leaf, bits, rank, inner, sizes, half),
        [
            out((rows, half), f32),
            out((rows, half), f32),
            out((bits * rank, half), f32),
            out((bits * rank, half), bf16),
        ],
        "front",
        6 * bits * rank * rows * samples,
        8 * levels * rows * rank,
        room=FRONT,
        ins=[SMEM, HBM, HBM, HBM, HBM],
        scratch=[
            pltpu.VMEM((rows, samples), bf16),
            pltpu.VMEM((rows, leaf), bf16),
            pltpu.VMEM((levels, rows, rank), f32),
            pltpu.VMEM((max(1, len(inner)), rows, rank), f32),
            pltpu.VMEM((bits * rank, rows), bf16),
            pltpu.VMEM((bits * rank, rows), bf16),
            pltpu.SemaphoreType.DMA((2 + levels + max(1, len(inner)),)),
        ],
    )(core_s, residual_cols, leaf_inverse, basis_right, basis_left)
    got = swapped(send, 1)
    solved_other = swapped(solved_send, 1)
    left16 = call(
        functools.partial(left_kernel, bits, rank),
        out((rows, bits * rank), bf16),
        "left16",
        bits * rows * rank,
        6 * bits * rows * rank,
        room=24,
        ins=[HBM],
        scratch=[pltpu.VMEM((bits, rows, rank), f32), pltpu.SemaphoreType.DMA((bits,))],
    )(basis_left)
    left_other = swapped(left16, 1)

    shares, others = [None] * bits, [None] * bits
    top = bits - 1
    depth_of = lambda bit: max(16, 1 << (bit - 1))
    pairs_below = lambda level: level * (level - 1) // 2 * rank
    spot_rows = jnp.concatenate([map_pos, spot_other]).reshape(1, 2 * tile)
    y, message = call(
        functools.partial(first_merge, top, rank, depth_of(1)),
        [
            out((top * rank, half), f32),
            out((top * rank + 3 * depth_of(1), half), bf16),
        ],
        "merge0",
        4 * top * rank * rank * half,
        8 * top * rank * half,
    )(keep, got, small, small_other, spot_rows)
    ahead = (1, 2)
    small_own, small_theirs = {}, {}
    previous = small, small_other
    for bit in ahead:
        kept = pairs_below(top - bit + 1)
        both = (previous[0][:kept].astype(f32) + previous[1][:kept].astype(f32)).astype(bf16)
        small_own[bit] = both
        small_theirs[bit] = swapped(both, 1 << bit)
        previous = small_own[bit], small_theirs[bit]
    shares[top] = got[top * rank :]
    last = keep[top * rank :].astype(bf16)
    others[top] = swapped(last, 1)
    points = [lax.dynamic_slice_in_dim(point_pos, s * rows, rows).reshape(blocks, leaf) for s in (me, me ^ 1)]
    points = jnp.concatenate(points, 0)
    info = jnp.concatenate(
        [me.reshape(1)]
        + [lax.dynamic_index_in_dim(t, s, 1, keepdims=False) for t in (block_first, block_count) for s in (me, me ^ 1)]
    )
    for bit in range(1, bits):
        level = top - bit
        arrived = swapped(message, 1 << bit)
        share = arrived[level * rank : (level + 1) * rank]
        shares[level] = share
        if level > 1:
            others[level] = swapped(share, 1)
        if level == 1:
            part_mine, part_other = call(
                functools.partial(partial_kernel, bits, rank),
                [out((rows, half), f32)] * 2,
                "partial",
                4 * bits * rows * rank * half,
                16 * rows * half,
            )(solved_mine, solved_other, left16, left_other, last, *shares[2:])
            arrived, part_mine, part_other, info, points = lax.optimization_barrier(
                (arrived, part_mine, part_other, info, points)
            )
        if level:
            apart, along = bit in ahead, bit + 1 not in ahead
            inner_rows = pairs_below(level) if along else 0
            *kept_y, message = call(
                functools.partial(
                    merge, level, rank, apart, along, 1 << (bit - 1), (depth_of(bit), depth_of(bit + 1))
                ),
                [out((level * rank, half), f32)] * (level > 1)
                + [out((level * rank + inner_rows + 3 * depth_of(bit + 1), half), bf16)],
                f"merge{bit}",
                4 * level * rank * rank * half,
                8 * level * rank * half,
            )(y, message, arrived, *((small_own[bit], small_theirs[bit]) if apart else ()))
            y = kept_y[0] if kept_y else None

    plane = 4
    near = devices // (4 * plane)
    depth = depth_of(bits - 1)
    chips = 1 << (bits - 2)
    near_weights = call(
        functools.partial(near_kernel, plane, near, tile, leaf, blocks, devices, chips, depth, rank),
        [out((2 * near * tile, 2 * rows), bf16)] * plane,
        "near",
        40 * plane * near * tile * rows,
        8 * plane * near * tile * rows,
        room=8 if near <= 4 else 24,
        ins=[SMEM, VMEM, VMEM],
    )(info, message, points)
    early_masks = (2, 3, 1)
    shape = plane, near, tile, leaf, blocks, devices
    final_mine, coeffs, spots, *partials = call(
        functools.partial(first_kernel, rank, chips, depth, 2.0 * leaf, early_masks, shape),
        [out((rows, half), f32), out((2 * rows, half), bf16), out((2 * tile, chips), f32)]
        + [out((4 * near * tile, half), bf16)] * len(early_masks),
        "first",
        64 * near * tile * rows * half,
        64 * near * tile * half,
        room=12 if near <= 4 else 28,
        ins=[SMEM] + [VMEM] * (7 + len(early_masks)),
        scratch=[pltpu.VMEM((2 * near * tile, 2 * rows), bf16)],
    )(
        info, points, part_mine, part_other, left16, left_other, shares[1], arrived,
        *[near_weights[mask] for mask in early_masks],
    )

    def weighed(mask, coeffs):
        return call(
            functools.partial(far_kernel, mask, *shape),
            out((4 * near * tile, half), bf16 if mask else f32),
            f"weigh{mask}",
            32 * near * tile * rows * half,
            32 * near * tile * half,
            room=8 if near <= 4 else 16,
            ins=[SMEM, VMEM, VMEM, VMEM, VMEM],
            scratch=[pltpu.VMEM((2 * near * tile, 2 * rows), bf16)],
        )(info, spots, near_weights[mask], points, coeffs)

    sent = [swapped(partial, mask << 1) for mask, partial in zip(early_masks, partials)]
    share0, share1, _ = lax.optimization_barrier((shares[0], shares[1], coeffs))
    others[:2] = swapped(share0, 1), swapped(share1, 1)
    solved_out = call(
        solved_kernel,
        out((rows, samples), f32),
        "solved",
        2 * bits * rows * rank * half,
        16 * rows * samples,
        ins=[SMEM] + [VMEM] * (3 + bits),
    )(core_s, final_mine, solved_send, left16, *others)
    coeffs, solved_out = lax.optimization_barrier((coeffs, solved_out))
    total = weighed(0, coeffs)
    for partial in sent:
        total = total + partial.astype(f32)
    far = 2 * near
    total = total.reshape(far, 2 * tile, half)
    result = total[0]
    for mask in reversed(range(1, far)):
        result = result + swapped(total[mask].astype(bf16), mask << 3).astype(f32)
    rest = swapped(result[tile:], 1)

    mapped = jnp.where(
        core == 0,
        jnp.concatenate([result[:tile], rest], 1),
        jnp.concatenate([rest, result[:tile]], 1),
    )
    return (solved_out, prior_map.astype(f32) + mapped)


def solution(mesh):
    in_specs = (
        P(("groups", "pts"), None),
        P(("groups", "pts"), None),
        P(None, ("groups", "pts"), None),
        P(None, ("groups", "pts"), None),
        P(),
        P("pts"),
        P(("groups", "pts"), None),
        P(),
        P(),
    )
    out_specs = (P(("groups", "pts"), None), P(("groups", "pts"), None))
    return jax.shard_map(body, mesh=mesh, in_specs=in_specs, out_specs=out_specs, check_vma=False)
```
